32 devices in a mesh: half: 2 (over x), panel: 4 (over y, core), dom: 4 (over z).
Axes of the slice: x: 2, y: 2, z: 4, core: 2. Of those that a mesh axis runs over, the one named last changes fastest.
Arguments:
- images: bfloat16 [512, 8192], P(('half', 'dom')), parts along dimension 0, may hold values from -128 to 128
- shift_index: int32 [512, 9], P(('half', 'dom')), parts along dimension 0, may hold values from 0 to 48, as said below
- references: bfloat16 [128, 8192], P(('half', 'panel', 'dom')), parts along dimension 0, may hold values from -0.6 to 0.6
- slot_blocks: int32 [128, 8], P(('half', 'panel')), parts along dimension 0, may hold values from 0 to 31
Outputs:
- volume: float32 [64, 1024], P(('half', 'panel', 'dom')), parts along dimension 0
- log_evidence: float32 [512], P(('half', 'dom')), parts along dimension 0
The draws below stay inside these ranges and needn't reach their ends.
There are 2 independent parts, one for each index of `half`. The reference program is written for one: setup_inputs(seed, part) draws one part's arguments, and reference() takes and returns one part's arrays. A program takes and returns all parts, laid end to end along the dimension named above; each array names one. Nothing has to cross between parts.
Inputs may be any that keep to these rules, and one draw needn't show every extreme that they name: `shift_index`: each row names 9 different offsets.
All inputs are finite; a program needn't handle non-finite values.
Results may differ from the reference program's by a relative error of at most 0.0048.
Values may be sent and summed in bfloat16 or wider, within the bound.
A program may use at most 128 MiB of HBM per device.

```python
import math
import jax
import jax.numpy as jnp
from jax import lax

PIX = 64
SHIFTS = 9
GRID = 7
SEG = 8
PARTICLES = 256
ORIENT = 64
VB = 32
BLK = 1024


def ref_rows(key):
    key_base, key_scale = jax.random.split(key)
    row_width = 2 * PIX * PIX
    values = jnp.clip(jax.random.normal(key_base, (ORIENT, row_width), jnp.float32), -6.0, 6.0)
    row_scale = jnp.exp(jax.random.uniform(key_scale, (ORIENT,), jnp.float32, math.log(0.5), math.log(1.5)))
    return values * row_scale[:, None] / PIX


def shift_rows(key):
    offset_count = GRID * GRID
    noise = jax.random.randint(key, (PARTICLES, offset_count), 0, 1 << 20)
    ranking = noise * offset_count + jnp.arange(offset_count, dtype=jnp.int32)[None, :]
    _, chosen = lax.top_k(ranking, SHIFTS)
    return chosen.astype(jnp.int32)


def draw_references(key, part):
    return ref_rows(jax.random.fold_in(key, 101)).astype(jnp.bfloat16)


def draw_shift_index(key, part):
    return shift_rows(jax.random.fold_in(key, 202))


def draw_images(key, part):
    row_width = 2 * PIX * PIX
    key_base = jax.random.fold_in(jax.random.fold_in(key, 303), 0)
    return jnp.clip(jax.random.normal(key_base, (PARTICLES, row_width), jnp.float32), -6.0, 6.0).astype(jnp.bfloat16)


def place_ends(drawn, stream_key, least, largest):
    dims = drawn.shape
    spot = [jax.random.randint(jax.random.fold_in(stream_key, axis), (), 0, dims[axis]) for axis in range(len(dims))]
    drawn = drawn.at[tuple(spot)].set(least)
    longest = dims.index(max(dims))
    spot[longest] = (spot[longest] + 1) % dims[longest]
    return drawn.at[tuple(spot)].set(largest)


def setup_inputs(seed: int = 0, part: int = 0) -> dict:
    key_list = jax.random.split(jax.random.key(seed), 5)
    part_splits = jax.random.split(jax.random.fold_in(key_list[4], part), 5)
    images = draw_images(jax.random.fold_in(jax.random.fold_in(key_list[4], part), 71), part)
    shift_index = draw_shift_index(jax.random.fold_in(jax.random.fold_in(key_list[4], part), 71), part)
    references = draw_references(jax.random.fold_in(jax.random.fold_in(key_list[4], part), 71), part)
    slot_blocks = place_ends(jax.random.randint(part_splits[3], (ORIENT, SEG), 0, VB), jax.random.fold_in(part_splits[3], 1), 0, VB - 1).astype(jnp.int32)
    return dict(images=images, shift_index=shift_index, references=references, slot_blocks=slot_blocks)


offset_sigma = 2.0


def offsets(shift_index):
    shift_row = (shift_index // GRID - GRID // 2).astype(jnp.float32)
    shift_col = (shift_index % GRID - GRID // 2).astype(jnp.float32)
    return shift_row, shift_col


def penalty(shift_index):
    shift_row, shift_col = offsets(shift_index)
    return (shift_row * shift_row + shift_col * shift_col) * (0.5 / (offset_sigma * offset_sigma))


def phase_table():
    shift_row, shift_col = offsets(jnp.arange(GRID * GRID, dtype=jnp.int32))
    frequency = jnp.arange(PIX, dtype=jnp.float32) - PIX // 2
    phase_angle = (-2.0 * math.pi / PIX) * (shift_row[:, None, None] * frequency[None, :, None] + shift_col[:, None, None] * frequency[None, None, :])
    return jnp.cos(phase_angle), jnp.sin(phase_angle)


def shift_images(images, shift_index, cos_table, sin_table):
    row_count = images.shape[0]
    cosine = cos_table[shift_index]
    sine_part = sin_table[shift_index]
    picture = images.astype(jnp.float32).reshape(row_count, 1, PIX, 2, PIX)
    real_part = picture[:, :, :, 0, :]
    imag_part = picture[:, :, :, 1, :]
    out_real = real_part * cosine - imag_part * sine_part
    out_imag = real_part * sine_part + imag_part * cosine
    return jnp.stack([out_real, out_imag], axis=3).reshape(row_count * SHIFTS, 2 * PIX * PIX).astype(jnp.bfloat16)


def reference(images, shift_index, references, slot_blocks):
    cos_table, sin_table = phase_table()
    block_size = math.gcd(PARTICLES, 64)
    block_count = PARTICLES // block_size
    ref_norms = jnp.sum(jnp.square(references.astype(jnp.float32)), axis=1)
    image_blocks = images.reshape(block_count, block_size, 2 * PIX * PIX)
    index_blocks = shift_index.reshape(block_count, block_size, SHIFTS)

    def one_block(blocks):
        image_block, index_block = blocks
        moved = shift_images(image_block, index_block, cos_table, sin_table)
        correlation = lax.dot_general(moved, references, (((1,), (1,)), ((), ())), preferred_element_type=jnp.float32)
        return correlation - 0.5 * ref_norms[None, :] - penalty(index_block).reshape(-1, 1)

    scores = lax.map(one_block, (image_blocks, index_blocks)).reshape(PARTICLES, SHIFTS * ORIENT)
    row_top = jnp.max(scores, axis=1)
    raised = jnp.exp(scores - row_top[:, None])
    row_total = jnp.sum(raised, axis=1)
    weights = (raised / row_total[:, None]).astype(jnp.bfloat16)
    log_evidence = row_top + jnp.log(row_total)
    weight_blocks = weights.reshape(block_count, block_size * SHIFTS, ORIENT)

    def add_block(running, inputs):
        image_block, index_block, weight_block = inputs
        moved = shift_images(image_block, index_block, cos_table, sin_table)
        return running + lax.dot_general(weight_block, moved, (((0,), (0,)), ((), ())), preferred_element_type=jnp.float32), None

    slab_sums, _ = lax.scan(add_block, jnp.zeros((ORIENT, 2 * PIX * PIX), jnp.float32), (image_blocks, index_blocks, weight_blocks))
    summed = jnp.zeros((VB, BLK), jnp.float32).at[slot_blocks.reshape(-1)].add(slab_sums.reshape(ORIENT * SEG, BLK))
    return summed * (PARTICLES * SEG / VB) ** -0.5, log_evidence
```

```python
import functools
import math

import jax
import jax.numpy as jnp
from jax import lax
from jax.experimental import pallas as pl
from jax.experimental.pallas import tpu as pltpu
from jax.sharding import PartitionSpec as P

MESH = pl.DeviceIdType.MESH
PIX = 64
SHIFTS = 9
LANES = 128
TILE = 16
T_GROUP = 3
U_BLOCK = 8
PENALTY = 0.125
F32 = jnp.float32
BF16 = jnp.bfloat16
NT = (((1,), (1,)), ((), ()))


def row_offset(index):
    return (index * 37) >> 8


def kernel(
    n_panel, n_dom, scale, images, shift, refs, slots, vol_out, log_out,
    img, refs32, gathered, norms, moved, slot_all, part32, part16, landed, logs,
    img_sem, recv_sem, z_sem, y_sem, sib_sem, slot_send, slot_recv,
    part_send, part_recv, log_send, log_recv,
):
    n = n_panel * n_dom
    n_y = n_panel // 2
    panel, dom = lax.axis_index("panel"), lax.axis_index("dom")
    me = panel * n_dom + dom
    rows = img.shape[0]
    ref_rows = refs.shape[0]
    pieces = TILE // ref_rows
    width = gathered.shape[1]
    cols = gathered.shape[0]
    segments = slots.shape[1]
    seg_len = moved.shape[1] // segments
    block_total = 2 * n
    core = lax.rem(panel, 2)
    sibling = panel + 1 - 2 * core

    def y_peer(step):
        return lax.rem(panel + 2 * step, n_panel)

    def place(d):
        return {"panel": lax.div(d, n_dom), "dom": lax.rem(d, n_dom)}

    barrier = pltpu.get_barrier_semaphore()

    @pl.loop(1, n)
    def _(o):
        pl.semaphore_signal(barrier, inc=1, device_id=place(lax.rem(me + o, n)), device_id_type=MESH)

    first = pl.multiple_of(panel * rows, rows)
    img_copy = pltpu.make_async_copy(images.at[pl.ds(first, rows), :], img, img_sem)
    img_copy.start()

    def shard(d):
        return gathered.at[pl.ds(pl.multiple_of(d * TILE, TILE), TILE), :]

    for q in range(pieces):
        refs32[q * ref_rows:(q + 1) * ref_rows, :] = refs[:, q * width:(q + 1) * width].astype(F32)
    gathered[pl.ds(pl.multiple_of(me * TILE, TILE), TILE), :] = refs32[...].astype(BF16)
    slot_rows = slots.shape[0]
    slot_all[pl.ds(pl.multiple_of(panel * slot_rows, slot_rows), slot_rows), :] = jnp.zeros(
        (slot_rows, LANES), jnp.int32
    )
    slot_all[pl.ds(pl.multiple_of(panel * slot_rows, slot_rows), slot_rows), :segments] = slots[...]

    pl.semaphore_wait(barrier, n - 1)

    def shard_copy(d, device, sem):
        return pltpu.make_async_remote_copy(
            src_ref=shard(d), dst_ref=shard(d), send_sem=sem, recv_sem=recv_sem.at[d],
            device_id=device, device_id_type=MESH,
        )

    def right_copy(j):
        return shard_copy(panel * n_dom + j, {"dom": dom + 1}, z_sem.at[0, j])

    def left_copy(j):
        return shard_copy(panel * n_dom + j, {"dom": dom - 1}, z_sem.at[1, j])

    def y_copy(step, j):
        return shard_copy(panel * n_dom + j, {"panel": y_peer(step)}, y_sem.at[step - 1, j])

    def sib_copy(d):
        return shard_copy(d, {"panel": sibling}, sib_sem.at[d])

    def relay(j):
        for step in range(1, n_y):
            y_copy(step, j).start()
        sib_copy(panel * n_dom + j).start()

    def from_left(s):
        j = dom - s

        @pl.when(j >= 0)
        def _():
            if s > 0:
                sib_copy(panel * n_dom + j).wait_recv()

            @pl.when(dom + 1 < n_dom)
            def _():
                right_copy(j).start()

            if s > 0:
                relay(j)

    def from_right(s):
        j = dom + s

        @pl.when(j < n_dom)
        def _():
            if s > 0:
                sib_copy(panel * n_dom + j).wait_recv()

            @pl.when(dom >= 1)
            def _():
                left_copy(j).start()

            relay(j)

    def from_y(s):
        for step in range(1, n_y):
            base = y_peer(step) * n_dom

            def pass_on(j):
                sib_copy(base + j).wait_recv()
                sib_copy(base + j).start()

            if s > 0:
                pl.when(dom - s >= 0)(lambda: pass_on(dom - s))
            pl.when(dom + s < n_dom)(lambda: pass_on(dom + s))

    def slot_copy(step):
        own = slot_all.at[pl.ds(pl.multiple_of(panel * slot_rows, slot_rows), slot_rows), :]
        return pltpu.make_async_remote_copy(
            src_ref=own, dst_ref=own, send_sem=slot_send.at[step - 1], recv_sem=slot_recv.at[panel],
            device_id={"panel": lax.rem(panel + step, n_panel)}, device_id_type=MESH,
        )

    from_left(0)
    from_right(0)
    for step in range(1, n_panel):
        slot_copy(step).start()

    lane = lax.broadcasted_iota(jnp.int32, (rows, LANES), 1)
    turn_sign = jnp.where(lane < PIX, -1.0, 1.0).astype(F32)
    freq_col = (lane & (PIX - 1)) - PIX // 2

    def offsets(t):
        index = shift[pl.ds(first, rows), t:t + 1]
        a = row_offset(index)
        return a - 3, index - 7 * a - 3

    def shift_group(t0):
        angles, steps = [], []
        for t in range(t0, t0 + T_GROUP):
            a, b = offsets(t)
            turns = ((freq_col * b - (PIX // 2) * a + PIX // 2) & (PIX - 1)) - PIX // 2
            angles.append(turns.astype(F32) * (-2.0 * math.pi / PIX))
            steps.append(jnp.broadcast_to(a, (rows, LANES)).astype(F32) * (-2.0 * math.pi / PIX))
        angle = jnp.concatenate(angles, axis=0)
        turn = jnp.concatenate(steps, axis=0)
        sign = jnp.concatenate([turn_sign] * T_GROUP, axis=0)
        turn_cos, turn_sin = jnp.cos(turn), jnp.sin(turn) * sign

        def body(block, carry):
            cosine, sine = carry
            for k in range(U_BLOCK):
                at = pl.multiple_of((block * U_BLOCK + k) * LANES, LANES)
                x = img[:, pl.ds(at, LANES)].astype(F32)
                swapped = pltpu.roll(x, PIX, 1)
                x = jnp.concatenate([x] * T_GROUP, axis=0)
                swapped = jnp.concatenate([swapped] * T_GROUP, axis=0)
                moved[t0 * rows:(t0 + T_GROUP) * rows, pl.ds(at, LANES)] = (
                    x * cosine + swapped * sine
                ).astype(BF16)
                cosine, sine = cosine * turn_cos - sine * turn_sin, sine * turn_cos + cosine * turn_sin
            return cosine, sine

        lax.fori_loop(0, PIX // U_BLOCK, body, (jnp.cos(angle), jnp.sin(angle) * sign))

    img_copy.wait()
    groups = list(range(0, SHIFTS, T_GROUP))
    shift_group(groups[0])
    for s in range(1, n_dom):
        from_left(s)
        from_right(s)
        from_y(s - 1)
        if s < len(groups):
            shift_group(groups[s])
    for t0 in groups[max(n_dom, 1):]:
        shift_group(t0)
    from_y(n_dom - 1)
    for step in range(n_y):
        base = lax.rem(sibling + 2 * step, n_panel) * n_dom
        for j in range(n_dom):
            sib_copy(base + j).wait_recv()

    @pl.loop(0, n)
    def _(d):
        at = pl.ds(pl.multiple_of(d * TILE, TILE), TILE)
        total = jnp.zeros((TILE, LANES), F32)
        for k in range(width // LANES):
            value = gathered[at, k * LANES:(k + 1) * LANES].astype(F32)
            total += value * value
        norms[at, :] = total

    def fold(q, value):
        return value if q == 0 else pltpu.roll(value, cols - q * ref_rows, 1)

    scores = jnp.zeros((SHIFTS * rows, cols), F32)
    half_norm = -0.5 * jnp.sum(jnp.transpose(norms[...]), axis=0, keepdims=True)
    half_norm = jnp.broadcast_to(half_norm, (8, cols))
    norm_row = jnp.zeros((8, cols), F32)
    for q in range(pieces):
        product = lax.dot_general(
            moved[:, q * width:(q + 1) * width], gathered[...], NT, preferred_element_type=F32
        )
        scores += fold(q, product)
        norm_row += fold(q, half_norm)
    column = lax.broadcasted_iota(jnp.int32, (rows, cols), 1)
    valid = (column & (TILE - 1)) < ref_rows
    blocks = []
    for t in range(SHIFTS):
        a, b = offsets(t)
        cost = (a * a + b * b).astype(F32) * PENALTY
        block = scores[t * rows:(t + 1) * rows] + norm_row[:1] - cost
        blocks.append(jnp.where(valid, block, -jnp.inf))
    top = functools.reduce(jnp.maximum, blocks)
    top = jnp.max(top, axis=1, keepdims=True)
    blocks = [jnp.exp(block - top) for block in blocks]
    total = jnp.sum(sum(blocks), axis=1, keepdims=True)
    inverse = 1.0 / total
    weights = jnp.concatenate([(block * inverse).astype(BF16) for block in blocks], axis=0)

    evidence = top + jnp.log(total)
    spot = lax.broadcasted_iota(jnp.int32, (rows, LANES), 0) + panel * rows
    log_row = jnp.sum(jnp.where(lane == spot, evidence, 0.0), axis=0, keepdims=True)
    logs[panel] = jnp.broadcast_to(log_row, (8, LANES))

    def log_copy(step):
        return pltpu.make_async_remote_copy(
            src_ref=logs.at[panel], dst_ref=logs.at[panel], send_sem=log_send.at[step - 1],
            recv_sem=log_recv.at[panel],
            device_id={"panel": lax.rem(panel + step, n_panel)}, device_id_type=MESH,
        )

    for step in range(1, n_panel):
        log_copy(step).start()

    for step in range(1, n_panel):
        sender = lax.rem(panel + step, n_panel)
        landing = slot_all.at[pl.ds(pl.multiple_of(sender * slot_rows, slot_rows), slot_rows), :]
        pltpu.make_async_remote_copy(
            src_ref=landing, dst_ref=landing, send_sem=slot_send.at[step - 1], recv_sem=slot_recv.at[sender],
            device_id={"panel": sender}, device_id_type=MESH,
        ).wait_recv()
    ref_total = slot_all.shape[0]
    spread_col = lax.broadcasted_iota(jnp.int32, (ref_total, cols), 1)
    spread_row = lax.broadcasted_iota(jnp.int32, (ref_total, cols), 0)
    within = spread_col & (TILE - 1)
    spread_to = jnp.where(within < ref_rows, (spread_col >> 4) * ref_rows + within, -1)
    spread = jnp.where(spread_row == spread_to, 1.0, 0.0).astype(BF16)
    slot_t = jnp.transpose(slot_all[...].astype(F32))[:TILE].astype(BF16)
    slot_of = jnp.dot(slot_t, spread, preferred_element_type=F32)
    block_id = lax.broadcasted_iota(jnp.int32, (block_total, cols), 0).astype(F32)
    owner_rows = []
    for s in range(segments):
        owner_rows.append(jnp.where(block_id == slot_of[s:s + 1], 1.0, 0.0).astype(BF16))
    onehot = jnp.concatenate(owner_rows, axis=0)
    mixed = lax.dot_general(onehot, weights, NT, preferred_element_type=F32).astype(BF16)

    chunk = 2 * LANES
    lines = seg_len // LANES
    for c in range(seg_len // chunk):
        total = jnp.zeros((block_total, chunk), F32)
        for s in range(segments):
            at = s * seg_len + c * chunk
            total += jnp.dot(
                mixed[s * block_total:(s + 1) * block_total], moved[:, at:at + chunk],
                preferred_element_type=F32,
            )
        for k in range(2):
            part32[pl.ds(2 * c + k, block_total, stride=lines), :] = total[:, k * LANES:(k + 1) * LANES]
    part16[...] = part32[...].astype(BF16)

    def tile_of(ref, d):
        return ref.at[pl.ds(pl.multiple_of(d * TILE, TILE), TILE), :]

    def part_copy(d):
        return pltpu.make_async_remote_copy(
            src_ref=tile_of(part16, d), dst_ref=tile_of(landed, me), send_sem=part_send.at[d],
            recv_sem=part_recv.at[me], device_id=place(d), device_id_type=MESH,
        )

    def part_landing(d):
        return pltpu.make_async_remote_copy(
            src_ref=tile_of(part16, d), dst_ref=tile_of(landed, d), send_sem=part_send.at[d],
            recv_sem=part_recv.at[d], device_id=place(d), device_id_type=MESH,
        )

    @pl.loop(1, n)
    def _(o):
        part_copy(lax.rem(me + o, n)).start()

    def add_part(o, total):
        d = lax.rem(me + o, n)
        part_landing(d).wait_recv()
        return total + landed[pl.ds(pl.multiple_of(d * TILE, TILE), TILE), :].astype(F32)

    total = part32[pl.ds(pl.multiple_of(me * TILE, TILE), TILE), :]
    total = lax.fori_loop(1, n, add_part, total) * scale
    for k in range(TILE):
        vol_out[k // lines:k // lines + 1, (k % lines) * LANES:(k % lines + 1) * LANES] = total[k:k + 1]

    log_total = logs[panel]
    for step in range(1, n_panel):
        sender = lax.rem(panel + step, n_panel)
        pltpu.make_async_remote_copy(
            src_ref=logs.at[sender], dst_ref=logs.at[sender], send_sem=log_send.at[step - 1],
            recv_sem=log_recv.at[sender], device_id={"panel": sender}, device_id_type=MESH,
        ).wait_recv()
        log_total += logs[sender]
    log_out[...] = log_total[:1, :log_out.shape[1]]

    @pl.loop(1, n)
    def _(o):
        part_copy(lax.rem(me + o, n)).wait_send()

    for step in range(1, n_panel):
        slot_copy(step).wait_send()
        log_copy(step).wait_send()
    for j in range(n_dom):
        @pl.when((j <= dom) & (dom + 1 < n_dom))
        def _():
            right_copy(j).wait_send()

        @pl.when((j >= dom) & (dom >= 1))
        def _():
            left_copy(j).wait_send()

        for step in range(1, n_y):
            y_copy(step, j).wait_send()
        for step in range(n_y):
            sib_copy(y_peer(step) * n_dom + j).wait_send()


def shards(images, shift_index, references, slot_blocks):
    n_panel = lax.axis_size("panel")
    n_dom = lax.axis_size("dom")
    n = n_panel * n_dom
    part_dev, row_width = images.shape
    segments = slot_blocks.shape[1]
    block_total = 2 * n
    volume_scale = (part_dev * n_dom * segments / block_total) ** (-0.5)
    rows = part_dev // n_panel
    width = row_width * references.shape[0] // TILE
    seg_len = row_width // segments
    lines = seg_len // LANES
    vmem = pl.BlockSpec(memory_space=pltpu.VMEM)
    dma = pltpu.SemaphoreType.DMA
    volume, log_evidence = pl.pallas_call(
        functools.partial(kernel, n_panel, n_dom, volume_scale),
        out_shape=(
            jax.ShapeDtypeStruct((2, seg_len), F32),
            jax.ShapeDtypeStruct((1, part_dev), F32),
        ),
        in_specs=[pl.BlockSpec(memory_space=pl.ANY), vmem, vmem, vmem],
        out_specs=(vmem, vmem),
        scratch_shapes=[
            pltpu.VMEM((rows, row_width), BF16),
            pltpu.VMEM((TILE, width), F32),
            pltpu.VMEM((n * TILE, width), BF16),
            pltpu.VMEM((n * TILE, LANES), F32),
            pltpu.VMEM((SHIFTS * rows, row_width), BF16),
            pltpu.VMEM((n_panel * slot_blocks.shape[0], LANES), jnp.int32),
            pltpu.VMEM((block_total * lines, LANES), F32),
            pltpu.VMEM((block_total * lines, LANES), BF16),
            pltpu.VMEM((n * TILE, LANES), BF16),
            pltpu.VMEM((n_panel, 8, LANES), F32),
            dma(()),
            dma((n,)),
            dma((2, n_dom)),
            dma((max(n_panel // 2 - 1, 1), n_dom)),
            dma((n,)),
            dma((n_panel,)),
            dma((n_panel,)),
            dma((n,)),
            dma((n,)),
            dma((n_panel,)),
            dma((n_panel,)),
        ],
        compiler_params=pltpu.CompilerParams(
            collective_id=0, has_side_effects=True, vmem_limit_bytes=48 * 1024 * 1024
        ),
        name="expectation_backprojection",
    )(images, shift_index, references, slot_blocks)
    return volume, log_evidence.reshape(part_dev)


def solution(mesh):
    in_specs = (
        P(("half", "dom"), None),
        P(("half", "dom"), None),
        P(("half", "panel", "dom"), None),
        P(("half", "panel"), None),
    )
    out_specs = (P(("half", "panel", "dom"), None), P(("half", "dom")))
    return jax.shard_map(shards, mesh=mesh, in_specs=in_specs, out_specs=out_specs, check_vma=False)
```

```python
import functools
import math

import jax
import jax.numpy as jnp
from jax import lax
from jax.experimental import pallas as pl
from jax.experimental.pallas import tpu as pltpu
from jax.sharding import PartitionSpec as P

MESH = pl.DeviceIdType.MESH
PIX = 64
SHIFTS = 9
LANES = 128
TILE = 16
T_GROUP = 3
U_BLOCK = 8
PENALTY = 0.125
F32 = jnp.float32
BF16 = jnp.bfloat16
NT = (((1,), (1,)), ((), ()))


def row_offset(index):
    return (index * 37) >> 8


def kernel(
    n_panel, n_dom, scale, images, shift, refs, slots, vol_out, log_out,
    img, refs_in, shift_in, shift_pad, shift_col, refs32, gathered, norms, moved, slot_in, slot_all, onehot,
    part32, part16, landed, logs, in_sem, recv_sem, z_sem, y_sem, sib_sem, slot_send, slot_recv,
    part_send, part_recv, log_send, log_recv,
):
    n = n_panel * n_dom
    n_y = n_panel // 2
    panel, dom = lax.axis_index("panel"), lax.axis_index("dom")
    me = panel * n_dom + dom
    rows = img.shape[0]
    ref_rows = refs.shape[0]
    pieces = TILE // ref_rows
    width = gathered.shape[1]
    cols = gathered.shape[0]
    cands = SHIFTS * rows
    segments = slots.shape[0]
    seg_len = img.shape[1] // segments
    block_total = 2 * n
    core = lax.rem(panel, 2)
    sibling = panel + 1 - 2 * core

    def y_peer(step):
        return lax.rem(panel + 2 * step, n_panel)

    def place(d):
        return {"panel": lax.div(d, n_dom), "dom": lax.rem(d, n_dom)}

    first = pl.multiple_of(panel * rows, rows)
    refs_copy = pltpu.make_async_copy(refs, refs_in, in_sem.at[0])
    img_copy = pltpu.make_async_copy(images.at[pl.ds(first, rows), :], img, in_sem.at[1])
    shift_copy = pltpu.make_async_copy(shift, shift_in, in_sem.at[2])
    slot_load = pltpu.make_async_copy(slots, slot_in, in_sem.at[3])
    refs_copy.start()
    shift_copy.start()
    slot_load.start()
    img_copy.start()

    barrier = pltpu.get_barrier_semaphore()

    @pl.loop(1, n)
    def _(o):
        pl.semaphore_signal(barrier, inc=1, device_id=place(lax.rem(me + o, n)), device_id_type=MESH)

    def shard(d):
        return gathered.at[pl.ds(pl.multiple_of(d * TILE, TILE), TILE), :]

    def add_norm(d):
        at = pl.ds(pl.multiple_of(d * TILE, TILE), TILE)
        total = jnp.zeros((TILE, LANES), F32)
        for k in range(width // LANES):
            value = gathered[at, k * LANES:(k + 1) * LANES].astype(F32)
            total += value * value
        norms[at, :] = total

    refs_copy.wait()
    for q in range(pieces):
        refs32[q * ref_rows:(q + 1) * ref_rows, :] = refs_in[:, q * width:(q + 1) * width].astype(F32)
    gathered[pl.ds(pl.multiple_of(me * TILE, TILE), TILE), :] = refs32[...].astype(BF16)
    slot_load.wait()
    slot_all[panel] = jnp.zeros((segments, LANES), jnp.int32)
    slot_all[panel, :, :slots.shape[1]] = slot_in[...]

    pl.semaphore_wait(barrier, n - 1)

    def shard_copy(d, device, sem):
        return pltpu.make_async_remote_copy(
            src_ref=shard(d), dst_ref=shard(d), send_sem=sem, recv_sem=recv_sem.at[d],
            device_id=device, device_id_type=MESH,
        )

    def right_copy(j):
        return shard_copy(panel * n_dom + j, {"dom": dom + 1}, z_sem.at[0, j])

    def left_copy(j):
        return shard_copy(panel * n_dom + j, {"dom": dom - 1}, z_sem.at[1, j])

    def y_copy(step, j):
        return shard_copy(panel * n_dom + j, {"panel": y_peer(step)}, y_sem.at[step - 1, j])

    def sib_copy(d):
        return shard_copy(d, {"panel": sibling}, sib_sem.at[d])

    def relay(j):
        for step in range(1, n_y):
            y_copy(step, j).start()
        sib_copy(panel * n_dom + j).start()

    def from_left(s):
        j = dom - s

        @pl.when(j >= 0)
        def _():
            if s > 0:
                sib_copy(panel * n_dom + j).wait_recv()

            @pl.when(dom + 1 < n_dom)
            def _():
                right_copy(j).start()

            if s > 0:
                relay(j)
                add_norm(panel * n_dom + j)

    def from_right(s):
        j = dom + s

        @pl.when(j < n_dom)
        def _():
            if s > 0:
                sib_copy(panel * n_dom + j).wait_recv()

            @pl.when(dom >= 1)
            def _():
                left_copy(j).start()

            relay(j)
            add_norm(panel * n_dom + j)

    def from_y(s):
        for step in range(1, n_y):
            base = y_peer(step) * n_dom

            def pass_on(j):
                sib_copy(base + j).wait_recv()
                sib_copy(base + j).start()
                add_norm(base + j)

            if s > 0:
                pl.when(dom - s >= 0)(lambda: pass_on(dom - s))
            pl.when(dom + s < n_dom)(lambda: pass_on(dom + s))

    def slot_copy(step):
        own = slot_all.at[panel]
        return pltpu.make_async_remote_copy(
            src_ref=own, dst_ref=own, send_sem=slot_send.at[step - 1], recv_sem=slot_recv.at[panel],
            device_id={"panel": lax.rem(panel + step, n_panel)}, device_id_type=MESH,
        )

    from_left(0)
    from_right(0)
    for step in range(1, n_panel):
        slot_copy(step).start()

    lane = lax.broadcasted_iota(jnp.int32, (rows, LANES), 1)
    turn_sign = jnp.where(lane < PIX, -1.0, 1.0).astype(F32)
    freq_col = (lane & (PIX - 1)) - PIX // 2

    shift_copy.wait()
    shift_pad[...] = jnp.zeros(shift_pad.shape, F32)
    shift_pad[:SHIFTS, :shift.shape[1]] = shift_in[...].astype(F32)
    shift_col[...] = jnp.transpose(shift_pad[...]).astype(jnp.int32)

    multiple = lax.broadcasted_iota(jnp.int32, (8, LANES), 0)
    turns = (freq_col[:8] * multiple + PIX // 2) & (PIX - 1)
    angle = (turns - PIX // 2).astype(F32) * (-2.0 * math.pi / PIX)
    cos_rows, sin_rows = jnp.cos(angle), jnp.sin(angle)

    def offsets(t):
        index = shift_col[pl.ds(first, rows), t:t + 1]
        a = row_offset(index)
        return a - 3, index - 7 * a - 3

    def pick(k, options):
        out = options[0]
        for i in range(1, len(options)):
            out = jnp.where(k == i, options[i], out)
        return out

    blocks_per_piece = width // (U_BLOCK * LANES)

    def shift_group(t0):
        parts = []
        for t in range(t0, t0 + T_GROUP):
            a, b = offsets(t)
            a = jnp.broadcast_to(a, (rows, LANES))
            b = jnp.broadcast_to(b, (rows, LANES))
            flip = jnp.where((a & 1) == 1, -1.0, 1.0).astype(F32)
            far_a, far_b = jnp.abs(a), jnp.abs(b)
            cosine = flip * pick(far_b, [cos_rows[k:k + 1] for k in range(4)])
            sine = flip * pick(far_b, [sin_rows[k:k + 1] for k in range(4)]) * turn_sign
            sine = jnp.where(b < 0, -sine, sine)
            turn_cos = pick(far_a, [jnp.full((rows, LANES), math.cos(2 * math.pi * k / PIX), F32) for k in range(4)])
            turn_sin = pick(far_a, [jnp.full((rows, LANES), math.sin(2 * math.pi * k / PIX), F32) for k in range(4)])
            turn_sin = jnp.where(a < 0, turn_sin, -turn_sin) * turn_sign
            parts.append((cosine, sine, turn_cos, turn_sin))
        cosine, sine, turn_cos, turn_sin = (jnp.concatenate(x, axis=0) for x in zip(*parts))

        def body(block, carry):
            cosine, sine = carry
            q = lax.div(block, blocks_per_piece)
            lane0 = lax.rem(block, blocks_per_piece) * (U_BLOCK * LANES)
            at_rows = pl.ds(pl.multiple_of(q * cands + t0 * rows, rows), T_GROUP * rows)
            for k in range(U_BLOCK):
                at = pl.multiple_of((block * U_BLOCK + k) * LANES, LANES)
                to = pl.multiple_of(lane0 + k * LANES, LANES)
                x = img[:, pl.ds(at, LANES)].astype(F32)
                swapped = pltpu.roll(x, PIX, 1)
                x = jnp.concatenate([x] * T_GROUP, axis=0)
                swapped = jnp.concatenate([swapped] * T_GROUP, axis=0)
                moved[at_rows, pl.ds(to, LANES)] = (x * cosine + swapped * sine).astype(BF16)
                cosine, sine = cosine * turn_cos - sine * turn_sin, sine * turn_cos + cosine * turn_sin
            return cosine, sine

        lax.fori_loop(0, PIX // U_BLOCK, body, (cosine, sine))

    def build_onehot():
        for step in range(1, n_panel):
            sender = lax.rem(panel + step, n_panel)
            pltpu.make_async_remote_copy(
                src_ref=slot_all.at[sender], dst_ref=slot_all.at[sender], send_sem=slot_send.at[step - 1],
                recv_sem=slot_recv.at[sender], device_id={"panel": sender}, device_id_type=MESH,
            ).wait_recv()
        spread_col = lax.broadcasted_iota(jnp.int32, (LANES, cols), 1)
        spread_row = lax.broadcasted_iota(jnp.int32, (LANES, cols), 0)
        within = spread_col & (TILE - 1)
        spread_to = jnp.where(within < ref_rows, (spread_col >> 4) * ref_rows + within, -1)
        slot_of = jnp.zeros((segments, cols), F32)
        for k in range(n_panel):
            spread = jnp.where(spread_row + k * slots.shape[1] == spread_to, 1.0, 0.0)
            spread = jnp.where(spread_row < slots.shape[1], spread, 0.0).astype(BF16)
            slot_of += jnp.dot(slot_all[k].astype(F32).astype(BF16), spread, preferred_element_type=F32)
        block_id = lax.broadcasted_iota(jnp.int32, (block_total, cols), 0).astype(F32)
        for s in range(segments):
            onehot[s * block_total:(s + 1) * block_total, :] = jnp.where(
                block_id == slot_of[s:s + 1], 1.0, 0.0
            ).astype(BF16)

    img_copy.wait()
    groups = list(range(0, SHIFTS, T_GROUP))
    shift_group(groups[0])
    for s in range(1, n_dom):
        from_left(s)
        from_right(s)
        from_y(s - 1)
        if s < len(groups):
            shift_group(groups[s])
        else:
            if s == len(groups):
                build_onehot()
    for t0 in groups[max(n_dom, 1):]:
        shift_group(t0)
    if n_dom <= len(groups):
        build_onehot()
    from_y(n_dom - 1)
    for step in range(n_y):
        base = lax.rem(sibling + 2 * step, n_panel) * n_dom
        for j in range(n_dom):
            sib_copy(base + j).wait_recv()
            add_norm(base + j)

    def fold(q, value):
        return value if q == 0 else pltpu.roll(value, cols - q * ref_rows, 1)

    scores = jnp.zeros((SHIFTS * rows, cols), F32)
    half_norm = -0.5 * jnp.sum(jnp.transpose(norms[...]), axis=0, keepdims=True)
    half_norm = jnp.broadcast_to(half_norm, (8, cols))
    norm_row = jnp.zeros((8, cols), F32)
    product = lax.dot_general(moved[...], gathered[...], NT, preferred_element_type=F32)
    for q in range(pieces):
        scores += fold(q, product[q * cands:(q + 1) * cands])
        norm_row += fold(q, half_norm)
    column = lax.broadcasted_iota(jnp.int32, (rows, cols), 1)
    valid = (column & (TILE - 1)) < ref_rows
    blocks = []
    for t in range(SHIFTS):
        a, b = offsets(t)
        cost = (a * a + b * b).astype(F32) * PENALTY
        block = scores[t * rows:(t + 1) * rows] + norm_row[:1] - cost
        blocks.append(jnp.where(valid, block, -jnp.inf))
    top = functools.reduce(jnp.maximum, blocks)
    top = jnp.max(top, axis=1, keepdims=True)
    blocks = [jnp.exp(block - top) for block in blocks]
    total = jnp.sum(sum(blocks), axis=1, keepdims=True)
    inverse = 1.0 / total
    weights = jnp.concatenate([(block * inverse).astype(BF16) for block in blocks], axis=0)

    evidence = top + jnp.log(total)
    spot = lax.broadcasted_iota(jnp.int32, (rows, LANES), 0) + panel * rows
    log_row = jnp.sum(jnp.where(lane == spot, evidence, 0.0), axis=0, keepdims=True)
    logs[panel] = jnp.broadcast_to(log_row, (8, LANES))

    def log_copy(step):
        return pltpu.make_async_remote_copy(
            src_ref=logs.at[panel], dst_ref=logs.at[panel], send_sem=log_send.at[step - 1],
            recv_sem=log_recv.at[panel],
            device_id={"panel": lax.rem(panel + step, n_panel)}, device_id_type=MESH,
        )

    for step in range(1, n_panel):
        log_copy(step).start()

    mixed = lax.dot_general(onehot[...], weights, NT, preferred_element_type=F32).astype(BF16)

    chunk = 2 * LANES
    lines = seg_len // LANES
    for c in range(seg_len // chunk):
        total = jnp.zeros((block_total, chunk), F32)
        for s in range(segments):
            q, at = divmod(s * seg_len + c * chunk, width)
            total += jnp.dot(
                mixed[s * block_total:(s + 1) * block_total], moved[q * cands:(q + 1) * cands, at:at + chunk],
                preferred_element_type=F32,
            )
        for k in range(2):
            part32[pl.ds(2 * c + k, block_total, stride=lines), :] = total[:, k * LANES:(k + 1) * LANES]
    part16[...] = part32[...].astype(BF16)

    def tile_of(ref, d):
        return ref.at[pl.ds(pl.multiple_of(d * TILE, TILE), TILE), :]

    def part_copy(d):
        return pltpu.make_async_remote_copy(
            src_ref=tile_of(part16, d), dst_ref=tile_of(landed, me), send_sem=part_send.at[d],
            recv_sem=part_recv.at[me], device_id=place(d), device_id_type=MESH,
        )

    def part_landing(d):
        return pltpu.make_async_remote_copy(
            src_ref=tile_of(part16, d), dst_ref=tile_of(landed, d), send_sem=part_send.at[d],
            recv_sem=part_recv.at[d], device_id=place(d), device_id_type=MESH,
        )

    @pl.loop(1, n)
    def _(o):
        part_copy(lax.rem(me + o, n)).start()

    def add_part(o, total):
        d = lax.rem(me + o, n)
        part_landing(d).wait_recv()
        return total + landed[pl.ds(pl.multiple_of(d * TILE, TILE), TILE), :].astype(F32)

    total = part32[pl.ds(pl.multiple_of(me * TILE, TILE), TILE), :]
    total = lax.fori_loop(1, n, add_part, total) * scale
    for k in range(TILE):
        vol_out[k // lines:k // lines + 1, (k % lines) * LANES:(k % lines + 1) * LANES] = total[k:k + 1]

    log_total = logs[panel]
    for step in range(1, n_panel):
        sender = lax.rem(panel + step, n_panel)
        pltpu.make_async_remote_copy(
            src_ref=logs.at[sender], dst_ref=logs.at[sender], send_sem=log_send.at[step - 1],
            recv_sem=log_recv.at[sender], device_id={"panel": sender}, device_id_type=MESH,
        ).wait_recv()
        log_total += logs[sender]
    log_out[...] = log_total[:1, :log_out.shape[1]]

    @pl.loop(1, n)
    def _(o):
        part_copy(lax.rem(me + o, n)).wait_send()

    for step in range(1, n_panel):
        slot_copy(step).wait_send()
        log_copy(step).wait_send()
    for j in range(n_dom):
        @pl.when((j <= dom) & (dom + 1 < n_dom))
        def _():
            right_copy(j).wait_send()

        @pl.when((j >= dom) & (dom >= 1))
        def _():
            left_copy(j).wait_send()

        for step in range(1, n_y):
            y_copy(step, j).wait_send()
        for step in range(n_y):
            sib_copy(y_peer(step) * n_dom + j).wait_send()


def shards(images, shift_index, references, slot_blocks):
    n_panel = lax.axis_size("panel")
    n_dom = lax.axis_size("dom")
    n = n_panel * n_dom
    part_dev, row_width = images.shape
    slot_rows, segments = slot_blocks.shape
    block_total = 2 * n
    volume_scale = (part_dev * n_dom * segments / block_total) ** (-0.5)
    rows = part_dev // n_panel
    width = row_width * references.shape[0] // TILE
    seg_len = row_width // segments
    lines = seg_len // LANES
    vmem = pl.BlockSpec(memory_space=pltpu.VMEM)
    dma = pltpu.SemaphoreType.DMA
    volume, log_evidence = pl.pallas_call(
        functools.partial(kernel, n_panel, n_dom, volume_scale),
        out_shape=(
            jax.ShapeDtypeStruct((2, seg_len), F32),
            jax.ShapeDtypeStruct((1, part_dev), F32),
        ),
        in_specs=[pl.BlockSpec(memory_space=pltpu.HBM)] * 4,
        out_specs=(vmem, vmem),
        scratch_shapes=[
            pltpu.VMEM((rows, row_width), BF16),
            pltpu.VMEM(references.shape, BF16),
            pltpu.VMEM((SHIFTS, part_dev), jnp.int32),
            pltpu.VMEM((TILE, LANES), F32),
            pltpu.VMEM((LANES, TILE), jnp.int32),
            pltpu.VMEM((TILE, width), F32),
            pltpu.VMEM((n * TILE, width), BF16),
            pltpu.VMEM((n * TILE, LANES), F32),
            pltpu.VMEM((SHIFTS * rows * (row_width // width), width), BF16),
            pltpu.VMEM((segments, slot_rows), jnp.int32),
            pltpu.VMEM((n_panel, segments, LANES), jnp.int32),
            pltpu.VMEM((segments * block_total, n * TILE), BF16),
            pltpu.VMEM((block_total * lines, LANES), F32),
            pltpu.VMEM((block_total * lines, LANES), BF16),
            pltpu.VMEM((n * TILE, LANES), BF16),
            pltpu.VMEM((n_panel, 8, LANES), F32),
            dma((4,)),
            dma((n,)),
            dma((2, n_dom)),
            dma((max(n_panel // 2 - 1, 1), n_dom)),
            dma((n,)),
            dma((n_panel,)),
            dma((n_panel,)),
            dma((n,)),
            dma((n,)),
            dma((n_panel,)),
            dma((n_panel,)),
        ],
        compiler_params=pltpu.CompilerParams(
            collective_id=0, has_side_effects=True, vmem_limit_bytes=56 * 1024 * 1024
        ),
        name="expectation_backprojection",
    )(images, shift_index.T, references, slot_blocks.T)
    return volume, log_evidence.reshape(part_dev)


def solution(mesh):
    in_specs = (
        P(("half", "dom"), None),
        P(("half", "dom"), None),
        P(("half", "panel", "dom"), None),
        P(("half", "panel"), None),
    )
    out_specs = (P(("half", "panel", "dom"), None), P(("half", "dom")))
    return jax.shard_map(shards, mesh=mesh, in_specs=in_specs, out_specs=out_specs, check_vma=False)
```

```python
import functools
import math

import jax
import jax.numpy as jnp
from jax import lax
from jax.experimental import pallas as pl
from jax.experimental.pallas import tpu as pltpu
from jax.sharding import PartitionSpec as P

MESH = pl.DeviceIdType.MESH
PIX = 64
SHIFTS = 9
LANES = 128
TILE = 16
T_GROUP = 3
U_BLOCK = 8
PENALTY = 0.125
F32 = jnp.float32
BF16 = jnp.bfloat16
NT = (((1,), (1,)), ((), ()))


def row_offset(index):
    return (index * 37) >> 8


def kernel(
    n_panel, n_dom, scale, images, shift, refs, slots, vol_out, log_out,
    img, refs_in, shift_in, shift_pad, shift_col, refs32, gathered, norms, moved, slot_in, slot_all, onehot,
    part32, part16, landed, logs, in_sem, recv_sem, z_sem, y_sem, sib_sem, slot_send, slot_recv,
    part_send, part_recv, log_send, log_recv,
):
    n = n_panel * n_dom
    n_y = n_panel // 2
    panel, dom = lax.axis_index("panel"), lax.axis_index("dom")
    me = panel * n_dom + dom
    rows = img.shape[0]
    ref_rows = refs.shape[0]
    pieces = TILE // ref_rows
    width = gathered.shape[1]
    cols = gathered.shape[0]
    cands = SHIFTS * rows
    segments = slots.shape[0]
    seg_len = img.shape[1] // segments
    block_total = 2 * n
    core = lax.rem(panel, 2)
    sibling = panel + 1 - 2 * core

    def y_peer(step):
        return lax.rem(panel + 2 * step, n_panel)

    def place(d):
        return {"panel": lax.div(d, n_dom), "dom": lax.rem(d, n_dom)}

    first = pl.multiple_of(panel * rows, rows)
    refs_copy = pltpu.make_async_copy(refs, refs_in, in_sem.at[0])
    img_copy = pltpu.make_async_copy(images.at[pl.ds(first, rows), :], img, in_sem.at[1])
    shift_copy = pltpu.make_async_copy(shift, shift_in, in_sem.at[2])
    slot_load = pltpu.make_async_copy(slots, slot_in, in_sem.at[3])
    refs_copy.start()
    shift_copy.start()
    slot_load.start()
    img_copy.start()

    barrier = pltpu.get_barrier_semaphore()

    @pl.loop(1, n_dom)
    def _(o):
        pl.semaphore_signal(
            barrier, inc=1, device_id={"dom": lax.rem(dom + o, n_dom)}, device_id_type=MESH
        )

    for step in range(1, n_panel):
        pl.semaphore_signal(
            barrier, inc=1, device_id={"panel": lax.rem(panel + step, n_panel)}, device_id_type=MESH
        )

    def shard(d):
        return gathered.at[pl.ds(pl.multiple_of(d * TILE, TILE), TILE), :]

    def add_norm(d):
        at = pl.ds(pl.multiple_of(d * TILE, TILE), TILE)
        total = jnp.zeros((TILE, LANES), F32)
        for k in range(width // LANES):
            value = gathered[at, k * LANES:(k + 1) * LANES].astype(F32)
            total += value * value
        norms[at, :] = total

    refs_copy.wait()
    for q in range(pieces):
        refs32[q * ref_rows:(q + 1) * ref_rows, :] = refs_in[:, q * width:(q + 1) * width].astype(F32)
    gathered[pl.ds(pl.multiple_of(me * TILE, TILE), TILE), :] = refs32[...].astype(BF16)
    slot_load.wait()
    slot_all[panel] = jnp.zeros((segments, LANES), jnp.int32)
    slot_all[panel, :, :slots.shape[1]] = slot_in[...]

    pl.semaphore_wait(barrier, n_dom + n_panel - 2)

    def shard_copy(d, device, sem):
        return pltpu.make_async_remote_copy(
            src_ref=shard(d), dst_ref=shard(d), send_sem=sem, recv_sem=recv_sem.at[d],
            device_id=device, device_id_type=MESH,
        )

    def line_copy(target):
        return shard_copy(me, {"dom": target}, z_sem.at[target])

    def y_copy(step, j):
        return shard_copy(panel * n_dom + j, {"panel": y_peer(step)}, y_sem.at[step - 1, j])

    def sib_copy(d):
        return shard_copy(d, {"panel": sibling}, sib_sem.at[d])

    def relay(j):
        for step in range(1, n_y):
            y_copy(step, j).start()
        sib_copy(panel * n_dom + j).start()

    def from_line(j):
        sib_copy(panel * n_dom + j).wait_recv()
        relay(j)
        add_norm(panel * n_dom + j)

    def at_distance(s, do):
        pl.when(dom - s >= 0)(lambda: do(dom - s))
        pl.when(dom + s < n_dom)(lambda: do(dom + s))

    def from_y(s):
        for step in range(1, n_y):
            base = y_peer(step) * n_dom

            def pass_on(j):
                sib_copy(base + j).wait_recv()
                sib_copy(base + j).start()
                add_norm(base + j)

            if s > 0:
                at_distance(s, pass_on)
            else:
                pass_on(dom)

    def slot_copy(step):
        own = slot_all.at[panel]
        return pltpu.make_async_remote_copy(
            src_ref=own, dst_ref=own, send_sem=slot_send.at[step - 1], recv_sem=slot_recv.at[panel],
            device_id={"panel": lax.rem(panel + step, n_panel)}, device_id_type=MESH,
        )

    relay(dom)
    for s in range(1, n_dom):
        at_distance(s, lambda target: line_copy(target).start())
    for step in range(1, n_panel):
        slot_copy(step).start()

    lane = lax.broadcasted_iota(jnp.int32, (rows, LANES), 1)
    turn_sign = jnp.where(lane < PIX, -1.0, 1.0).astype(F32)
    freq_col = (lane & (PIX - 1)) - PIX // 2

    shift_copy.wait()
    shift_pad[...] = jnp.zeros(shift_pad.shape, F32)
    shift_pad[:SHIFTS, :shift.shape[1]] = shift_in[...].astype(F32)
    shift_col[...] = jnp.transpose(shift_pad[...]).astype(jnp.int32)

    multiple = lax.broadcasted_iota(jnp.int32, (8, LANES), 0)
    turns = (freq_col[:8] * multiple + PIX // 2) & (PIX - 1)
    angle = (turns - PIX // 2).astype(F32) * (-2.0 * math.pi / PIX)
    cos_rows, sin_rows = jnp.cos(angle), jnp.sin(angle)

    def offsets(t):
        index = shift_col[pl.ds(first, rows), t:t + 1]
        a = row_offset(index)
        return a - 3, index - 7 * a - 3

    def pick(k, options):
        out = options[0]
        for i in range(1, len(options)):
            out = jnp.where(k == i, options[i], out)
        return out

    blocks_per_piece = width // (U_BLOCK * LANES)

    def shift_group(t0):
        parts = []
        for t in range(t0, t0 + T_GROUP):
            a, b = offsets(t)
            a = jnp.broadcast_to(a, (rows, LANES))
            b = jnp.broadcast_to(b, (rows, LANES))
            flip = jnp.where((a & 1) == 1, -1.0, 1.0).astype(F32)
            far_a, far_b = jnp.abs(a), jnp.abs(b)
            cosine = flip * pick(far_b, [cos_rows[k:k + 1] for k in range(4)])
            sine = flip * pick(far_b, [sin_rows[k:k + 1] for k in range(4)]) * turn_sign
            sine = jnp.where(b < 0, -sine, sine)
            turn_cos = pick(far_a, [jnp.full((rows, LANES), math.cos(2 * math.pi * k / PIX), F32) for k in range(4)])
            turn_sin = pick(far_a, [jnp.full((rows, LANES), math.sin(2 * math.pi * k / PIX), F32) for k in range(4)])
            turn_sin = jnp.where(a < 0, turn_sin, -turn_sin) * turn_sign
            parts.append((cosine, sine, turn_cos, turn_sin))
        cosine, sine, turn_cos, turn_sin = (jnp.concatenate(x, axis=0) for x in zip(*parts))

        def body(block, carry):
            cosine, sine = carry
            q = lax.div(block, blocks_per_piece)
            lane0 = lax.rem(block, blocks_per_piece) * (U_BLOCK * LANES)
            at_rows = pl.ds(pl.multiple_of(q * cands + t0 * rows, rows), T_GROUP * rows)
            for k in range(U_BLOCK):
                at = pl.multiple_of((block * U_BLOCK + k) * LANES, LANES)
                to = pl.multiple_of(lane0 + k * LANES, LANES)
                x = img[:, pl.ds(at, LANES)].astype(F32)
                swapped = pltpu.roll(x, PIX, 1)
                x = jnp.concatenate([x] * T_GROUP, axis=0)
                swapped = jnp.concatenate([swapped] * T_GROUP, axis=0)
                moved[at_rows, pl.ds(to, LANES)] = (x * cosine + swapped * sine).astype(BF16)
                cosine, sine = cosine * turn_cos - sine * turn_sin, sine * turn_cos + cosine * turn_sin
            return cosine, sine

        lax.fori_loop(0, PIX // U_BLOCK, body, (cosine, sine))

    def build_onehot():
        for step in range(1, n_panel):
            sender = lax.rem(panel + step, n_panel)
            pltpu.make_async_remote_copy(
                src_ref=slot_all.at[sender], dst_ref=slot_all.at[sender], send_sem=slot_send.at[step - 1],
                recv_sem=slot_recv.at[sender], device_id={"panel": sender}, device_id_type=MESH,
            ).wait_recv()
        spread_col = lax.broadcasted_iota(jnp.int32, (LANES, cols), 1)
        spread_row = lax.broadcasted_iota(jnp.int32, (LANES, cols), 0)
        within = spread_col & (TILE - 1)
        spread_to = jnp.where(within < ref_rows, (spread_col >> 4) * ref_rows + within, -1)
        slot_of = jnp.zeros((segments, cols), F32)
        for k in range(n_panel):
            spread = jnp.where(spread_row + k * slots.shape[1] == spread_to, 1.0, 0.0)
            spread = jnp.where(spread_row < slots.shape[1], spread, 0.0).astype(BF16)
            slot_of += jnp.dot(slot_all[k].astype(F32).astype(BF16), spread, preferred_element_type=F32)
        block_id = lax.broadcasted_iota(jnp.int32, (block_total, cols), 0).astype(F32)
        for s in range(segments):
            onehot[s * block_total:(s + 1) * block_total, :] = jnp.where(
                block_id == slot_of[s:s + 1], 1.0, 0.0
            ).astype(BF16)

    img_copy.wait()
    for t0 in range(0, SHIFTS, T_GROUP):
        shift_group(t0)
    add_norm(me)
    for s in range(1, n_dom):
        at_distance(s, from_line)
        from_y(s - 1)
        if s == 1:
            build_onehot()
    if n_dom == 1:
        build_onehot()
    from_y(n_dom - 1)
    for step in range(n_y):
        base = lax.rem(sibling + 2 * step, n_panel) * n_dom
        for j in range(n_dom):
            sib_copy(base + j).wait_recv()
            add_norm(base + j)

    def fold(q, value):
        return value if q == 0 else pltpu.roll(value, cols - q * ref_rows, 1)

    scores = jnp.zeros((SHIFTS * rows, cols), F32)
    half_norm = -0.5 * jnp.sum(jnp.transpose(norms[...]), axis=0, keepdims=True)
    half_norm = jnp.broadcast_to(half_norm, (8, cols))
    norm_row = jnp.zeros((8, cols), F32)
    product = lax.dot_general(moved[...], gathered[...], NT, preferred_element_type=F32)
    for q in range(pieces):
        scores += fold(q, product[q * cands:(q + 1) * cands])
        norm_row += fold(q, half_norm)
    column = lax.broadcasted_iota(jnp.int32, (rows, cols), 1)
    valid = (column & (TILE - 1)) < ref_rows
    blocks = []
    for t in range(SHIFTS):
        a, b = offsets(t)
        cost = (a * a + b * b).astype(F32) * PENALTY
        block = scores[t * rows:(t + 1) * rows] + norm_row[:1] - cost
        blocks.append(jnp.where(valid, block, -jnp.inf))
    top = functools.reduce(jnp.maximum, blocks)
    top = jnp.max(top, axis=1, keepdims=True)
    blocks = [jnp.exp(block - top) for block in blocks]
    total = jnp.sum(sum(blocks), axis=1, keepdims=True)
    inverse = 1.0 / total
    weights = jnp.concatenate([(block * inverse).astype(BF16) for block in blocks], axis=0)

    evidence = top + jnp.log(total)
    spot = lax.broadcasted_iota(jnp.int32, (rows, LANES), 0) + panel * rows
    log_row = jnp.sum(jnp.where(lane == spot, evidence, 0.0), axis=0, keepdims=True)
    logs[panel] = jnp.broadcast_to(log_row, (8, LANES))

    def log_copy(step):
        return pltpu.make_async_remote_copy(
            src_ref=logs.at[panel], dst_ref=logs.at[panel], send_sem=log_send.at[step - 1],
            recv_sem=log_recv.at[panel],
            device_id={"panel": lax.rem(panel + step, n_panel)}, device_id_type=MESH,
        )

    for step in range(1, n_panel):
        log_copy(step).start()

    mixed = lax.dot_general(onehot[...], weights, NT, preferred_element_type=F32).astype(BF16)

    chunk = 2 * LANES
    lines = seg_len // LANES
    for c in range(seg_len // chunk):
        total = jnp.zeros((block_total, chunk), F32)
        for s in range(segments):
            q, at = divmod(s * seg_len + c * chunk, width)
            total += jnp.dot(
                mixed[s * block_total:(s + 1) * block_total], moved[q * cands:(q + 1) * cands, at:at + chunk],
                preferred_element_type=F32,
            )
        for k in range(2):
            part32[pl.ds(2 * c + k, block_total, stride=lines), :] = total[:, k * LANES:(k + 1) * LANES]
    part16[...] = part32[...].astype(BF16)

    def tile_of(ref, d):
        return ref.at[pl.ds(pl.multiple_of(d * TILE, TILE), TILE), :]

    def part_copy(d):
        return pltpu.make_async_remote_copy(
            src_ref=tile_of(part16, d), dst_ref=tile_of(landed, me), send_sem=part_send.at[d],
            recv_sem=part_recv.at[me], device_id=place(d), device_id_type=MESH,
        )

    def part_landing(d):
        return pltpu.make_async_remote_copy(
            src_ref=tile_of(part16, d), dst_ref=tile_of(landed, d), send_sem=part_send.at[d],
            recv_sem=part_recv.at[d], device_id=place(d), device_id_type=MESH,
        )

    @pl.loop(1, n)
    def _(o):
        part_copy(lax.rem(me + o, n)).start()

    def add_part(o, total):
        d = lax.rem(me + o, n)
        part_landing(d).wait_recv()
        return total + landed[pl.ds(pl.multiple_of(d * TILE, TILE), TILE), :].astype(F32)

    total = part32[pl.ds(pl.multiple_of(me * TILE, TILE), TILE), :]
    total = lax.fori_loop(1, n, add_part, total) * scale
    for k in range(TILE):
        vol_out[k // lines:k // lines + 1, (k % lines) * LANES:(k % lines + 1) * LANES] = total[k:k + 1]

    log_total = logs[panel]
    for step in range(1, n_panel):
        sender = lax.rem(panel + step, n_panel)
        pltpu.make_async_remote_copy(
            src_ref=logs.at[sender], dst_ref=logs.at[sender], send_sem=log_send.at[step - 1],
            recv_sem=log_recv.at[sender], device_id={"panel": sender}, device_id_type=MESH,
        ).wait_recv()
        log_total += logs[sender]
    log_out[...] = log_total[:1, :log_out.shape[1]]

    @pl.loop(1, n)
    def _(o):
        part_copy(lax.rem(me + o, n)).wait_send()

    for step in range(1, n_panel):
        slot_copy(step).wait_send()
        log_copy(step).wait_send()
    for j in range(n_dom):
        @pl.when(j != dom)
        def _():
            line_copy(j).wait_send()

        for step in range(1, n_y):
            y_copy(step, j).wait_send()
        for step in range(n_y):
            sib_copy(y_peer(step) * n_dom + j).wait_send()


def shards(images, shift_index, references, slot_blocks):
    n_panel = lax.axis_size("panel")
    n_dom = lax.axis_size("dom")
    n = n_panel * n_dom
    part_dev, row_width = images.shape
    slot_rows, segments = slot_blocks.shape
    block_total = 2 * n
    volume_scale = (part_dev * n_dom * segments / block_total) ** (-0.5)
    rows = part_dev // n_panel
    width = row_width * references.shape[0] // TILE
    seg_len = row_width // segments
    lines = seg_len // LANES
    vmem = pl.BlockSpec(memory_space=pltpu.VMEM)
    dma = pltpu.SemaphoreType.DMA
    volume, log_evidence = pl.pallas_call(
        functools.partial(kernel, n_panel, n_dom, volume_scale),
        out_shape=(
            jax.ShapeDtypeStruct((2, seg_len), F32),
            jax.ShapeDtypeStruct((1, part_dev), F32),
        ),
        in_specs=[pl.BlockSpec(memory_space=pltpu.HBM)] * 4,
        out_specs=(vmem, vmem),
        scratch_shapes=[
            pltpu.VMEM((rows, row_width), BF16),
            pltpu.VMEM(references.shape, BF16),
            pltpu.VMEM((SHIFTS, part_dev), jnp.int32),
            pltpu.VMEM((TILE, LANES), F32),
            pltpu.VMEM((LANES, TILE), jnp.int32),
            pltpu.VMEM((TILE, width), F32),
            pltpu.VMEM((n * TILE, width), BF16),
            pltpu.VMEM((n * TILE, LANES), F32),
            pltpu.VMEM((SHIFTS * rows * (row_width // width), width), BF16),
            pltpu.VMEM((segments, slot_rows), jnp.int32),
            pltpu.VMEM((n_panel, segments, LANES), jnp.int32),
            pltpu.VMEM((segments * block_total, n * TILE), BF16),
            pltpu.VMEM((block_total * lines, LANES), F32),
            pltpu.VMEM((block_total * lines, LANES), BF16),
            pltpu.VMEM((n * TILE, LANES), BF16),
            pltpu.VMEM((n_panel, 8, LANES), F32),
            dma((4,)),
            dma((n,)),
            dma((n_dom,)),
            dma((max(n_panel // 2 - 1, 1), n_dom)),
            dma((n,)),
            dma((n_panel,)),
            dma((n_panel,)),
            dma((n,)),
            dma((n,)),
            dma((n_panel,)),
            dma((n_panel,)),
        ],
        compiler_params=pltpu.CompilerParams(
            collective_id=0, has_side_effects=True, vmem_limit_bytes=56 * 1024 * 1024
        ),
        name="expectation_backprojection",
    )(images, shift_index.T, references, slot_blocks.T)
    return volume, log_evidence.reshape(part_dev)


def solution(mesh):
    in_specs = (
        P(("half", "dom"), None),
        P(("half", "dom"), None),
        P(("half", "panel", "dom"), None),
        P(("half", "panel"), None),
    )
    out_specs = (P(("half", "panel", "dom"), None), P(("half", "dom")))
    return jax.shard_map(shards, mesh=mesh, in_specs=in_specs, out_specs=out_specs, check_vma=False)
```

```python
import functools
import math

import jax
import jax.numpy as jnp
from jax import lax
from jax.experimental import pallas as pl
from jax.experimental.pallas import tpu as pltpu
from jax.sharding import PartitionSpec as P

MESH = pl.DeviceIdType.MESH
PIX = 64
SHIFTS = 9
LANES = 128
TILE = 16
T_GROUP = 3
U_BLOCK = 8
PENALTY = 0.125
F32 = jnp.float32
BF16 = jnp.bfloat16
NT = (((1,), (1,)), ((), ()))


def row_offset(index):
    return (index * 37) >> 8


def kernel(
    n_panel, n_dom, scale, images, shift, refs, slots, vol_out, log_out,
    img, refs_in, shift_in, shift_pad, shift_col, refs32, gathered, norms, moved, slot_in, slot_all, onehot,
    part32, part16, landed, logs, in_sem, recv_sem, z_sem, far_sem, y_sem, sib_sem, slot_send, slot_recv,
    part_send, part_recv, log_send, log_recv,
):
    n = n_panel * n_dom
    n_y = n_panel // 2
    panel, dom = lax.axis_index("panel"), lax.axis_index("dom")
    me = panel * n_dom + dom
    rows = img.shape[0]
    ref_rows = refs.shape[0]
    pieces = TILE // ref_rows
    width = gathered.shape[1]
    cols = gathered.shape[0]
    cands = SHIFTS * rows
    segments = slots.shape[0]
    seg_len = img.shape[1] // segments
    block_total = 2 * n
    core = lax.rem(panel, 2)
    sibling = panel + 1 - 2 * core

    def y_peer(step):
        return lax.rem(panel + 2 * step, n_panel)

    def place(d):
        return {"panel": lax.div(d, n_dom), "dom": lax.rem(d, n_dom)}

    barrier = pltpu.get_barrier_semaphore()

    @pl.loop(1, n_dom)
    def _(o):
        pl.semaphore_signal(
            barrier, inc=1, device_id={"dom": lax.rem(dom + o, n_dom)}, device_id_type=MESH
        )

    for step in range(1, n_panel):
        pl.semaphore_signal(
            barrier, inc=1, device_id={"panel": lax.rem(panel + step, n_panel)}, device_id_type=MESH
        )

    for step in range(1, n_y):
        pl.semaphore_signal(
            barrier, inc=1, device_id={"panel": y_peer(step), "dom": n_dom - 1 - dom}, device_id_type=MESH
        )

    first = pl.multiple_of(panel * rows, rows)
    refs_copy = pltpu.make_async_copy(refs, refs_in, in_sem.at[0])
    img_copy = pltpu.make_async_copy(images.at[pl.ds(first, rows), :], img, in_sem.at[1])
    shift_copy = pltpu.make_async_copy(shift, shift_in, in_sem.at[2])
    slot_load = pltpu.make_async_copy(slots, slot_in, in_sem.at[3])
    refs_copy.start()
    shift_copy.start()
    slot_load.start()
    img_copy.start()

    def shard(d):
        return gathered.at[pl.ds(pl.multiple_of(d * TILE, TILE), TILE), :]

    def add_norm(d):
        at = pl.ds(pl.multiple_of(d * TILE, TILE), TILE)
        total = jnp.zeros((TILE, LANES), F32)
        for k in range(width // LANES):
            value = gathered[at, k * LANES:(k + 1) * LANES].astype(F32)
            total += value * value
        norms[at, :] = total

    refs_copy.wait()
    for q in range(pieces):
        refs32[q * ref_rows:(q + 1) * ref_rows, :] = refs_in[:, q * width:(q + 1) * width].astype(F32)
    gathered[pl.ds(pl.multiple_of(me * TILE, TILE), TILE), :] = refs32[...].astype(BF16)
    slot_load.wait()
    slot_all[panel] = jnp.zeros((segments, LANES), jnp.int32)
    slot_all[panel, :, :slots.shape[1]] = slot_in[...]

    pl.semaphore_wait(barrier, n_dom + n_panel + n_y - 3)

    def shard_copy(d, device, sem):
        return pltpu.make_async_remote_copy(
            src_ref=shard(d), dst_ref=shard(d), send_sem=sem, recv_sem=recv_sem.at[d],
            device_id=device, device_id_type=MESH,
        )

    def line_copy(target):
        return shard_copy(me, {"dom": target}, z_sem.at[target])

    def far_copy(step):
        return shard_copy(me, {"panel": y_peer(step), "dom": n_dom - 1 - dom}, far_sem.at[step - 1])

    def y_copy(step, j):
        return shard_copy(panel * n_dom + j, {"panel": y_peer(step)}, y_sem.at[step - 1, j])

    def sib_copy(d):
        return shard_copy(d, {"panel": sibling}, sib_sem.at[d])

    far = n_dom - 1
    at_end = (dom == 0) | (dom == far)

    def relay(j, across=True):
        if across:
            for step in range(1, n_y):
                y_copy(step, j).start()
        sib_copy(panel * n_dom + j).start()

    def from_line(j, across):
        sib_copy(panel * n_dom + j).wait_recv()
        relay(j, across)
        add_norm(panel * n_dom + j)

    def at_distance(s, do):
        pl.when(dom - s >= 0)(lambda: do(dom - s))
        pl.when(dom + s < n_dom)(lambda: do(dom + s))

    def from_y(s):
        for step in range(1, n_y):
            base = y_peer(step) * n_dom

            def pass_on(j):
                sib_copy(base + j).wait_recv()
                sib_copy(base + j).start()
                add_norm(base + j)

            if s > 0:
                at_distance(s, pass_on)
            else:
                pass_on(dom)

    def slot_copy(step):
        own = slot_all.at[panel]
        return pltpu.make_async_remote_copy(
            src_ref=own, dst_ref=own, send_sem=slot_send.at[step - 1], recv_sem=slot_recv.at[panel],
            device_id={"panel": lax.rem(panel + step, n_panel)}, device_id_type=MESH,
        )

    for s in range(1, n_dom):
        at_distance(s, lambda target: line_copy(target).start())
        if s == 1:
            for step in range(1, n_y):
                y_copy(step, dom).start()

    @pl.when(at_end)
    def _():
        for step in range(1, n_y):
            far_copy(step).start()

    sib_copy(me).start()
    for step in range(1, n_panel):
        slot_copy(step).start()

    lane = lax.broadcasted_iota(jnp.int32, (rows, LANES), 1)
    turn_sign = jnp.where(lane < PIX, -1.0, 1.0).astype(F32)
    freq_col = (lane & (PIX - 1)) - PIX // 2

    shift_copy.wait()
    shift_pad[...] = jnp.zeros(shift_pad.shape, F32)
    shift_pad[:SHIFTS, :shift.shape[1]] = shift_in[...].astype(F32)
    shift_col[...] = jnp.transpose(shift_pad[...]).astype(jnp.int32)

    multiple = lax.broadcasted_iota(jnp.int32, (8, LANES), 0)
    turns = (freq_col[:8] * multiple + PIX // 2) & (PIX - 1)
    angle = (turns - PIX // 2).astype(F32) * (-2.0 * math.pi / PIX)
    cos_rows, sin_rows = jnp.cos(angle), jnp.sin(angle)

    def offsets(t):
        index = shift_col[pl.ds(first, rows), t:t + 1]
        a = row_offset(index)
        return a - 3, index - 7 * a - 3

    def pick(k, options):
        out = options[0]
        for i in range(1, len(options)):
            out = jnp.where(k == i, options[i], out)
        return out

    blocks_per_piece = width // (U_BLOCK * LANES)

    def shift_group(t0):
        parts = []
        for t in range(t0, t0 + T_GROUP):
            a, b = offsets(t)
            a = jnp.broadcast_to(a, (rows, LANES))
            b = jnp.broadcast_to(b, (rows, LANES))
            flip = jnp.where((a & 1) == 1, -1.0, 1.0).astype(F32)
            far_a, far_b = jnp.abs(a), jnp.abs(b)
            cosine = flip * pick(far_b, [cos_rows[k:k + 1] for k in range(4)])
            sine = flip * pick(far_b, [sin_rows[k:k + 1] for k in range(4)]) * turn_sign
            sine = jnp.where(b < 0, -sine, sine)
            turn_cos = pick(far_a, [jnp.full((rows, LANES), math.cos(2 * math.pi * k / PIX), F32) for k in range(4)])
            turn_sin = pick(far_a, [jnp.full((rows, LANES), math.sin(2 * math.pi * k / PIX), F32) for k in range(4)])
            turn_sin = jnp.where(a < 0, turn_sin, -turn_sin) * turn_sign
            parts.append((cosine, sine, turn_cos, turn_sin))
        cosine, sine, turn_cos, turn_sin = (jnp.concatenate(x, axis=0) for x in zip(*parts))

        def body(block, carry):
            cosine, sine = carry
            q = lax.div(block, blocks_per_piece)
            lane0 = lax.rem(block, blocks_per_piece) * (U_BLOCK * LANES)
            at_rows = pl.ds(pl.multiple_of(q * cands + t0 * rows, rows), T_GROUP * rows)
            for k in range(U_BLOCK):
                at = pl.multiple_of((block * U_BLOCK + k) * LANES, LANES)
                to = pl.multiple_of(lane0 + k * LANES, LANES)
                x = img[:, pl.ds(at, LANES)].astype(F32)
                swapped = pltpu.roll(x, PIX, 1)
                x = jnp.concatenate([x] * T_GROUP, axis=0)
                swapped = jnp.concatenate([swapped] * T_GROUP, axis=0)
                moved[at_rows, pl.ds(to, LANES)] = (x * cosine + swapped * sine).astype(BF16)
                cosine, sine = cosine * turn_cos - sine * turn_sin, sine * turn_cos + cosine * turn_sin
            return cosine, sine

        lax.fori_loop(0, PIX // U_BLOCK, body, (cosine, sine))

    def build_onehot():
        for step in range(1, n_panel):
            sender = lax.rem(panel + step, n_panel)
            pltpu.make_async_remote_copy(
                src_ref=slot_all.at[sender], dst_ref=slot_all.at[sender], send_sem=slot_send.at[step - 1],
                recv_sem=slot_recv.at[sender], device_id={"panel": sender}, device_id_type=MESH,
            ).wait_recv()
        spread_col = lax.broadcasted_iota(jnp.int32, (LANES, cols), 1)
        spread_row = lax.broadcasted_iota(jnp.int32, (LANES, cols), 0)
        within = spread_col & (TILE - 1)
        spread_to = jnp.where(within < ref_rows, (spread_col >> 4) * ref_rows + within, -1)
        slot_of = jnp.zeros((segments, cols), F32)
        for k in range(n_panel):
            spread = jnp.where(spread_row + k * slots.shape[1] == spread_to, 1.0, 0.0)
            spread = jnp.where(spread_row < slots.shape[1], spread, 0.0).astype(BF16)
            slot_of += jnp.dot(slot_all[k].astype(F32).astype(BF16), spread, preferred_element_type=F32)
        block_id = lax.broadcasted_iota(jnp.int32, (block_total, cols), 0).astype(F32)
        for s in range(segments):
            onehot[s * block_total:(s + 1) * block_total, :] = jnp.where(
                block_id == slot_of[s:s + 1], 1.0, 0.0
            ).astype(BF16)

    img_copy.wait()
    for t0 in range(0, SHIFTS, T_GROUP):
        shift_group(t0)
    add_norm(me)
    for s in range(1, n_dom):
        at_distance(s, functools.partial(from_line, across=s < far))
        from_y(s - 1)
        if s == 1:
            build_onehot()
    if n_dom == 1:
        build_onehot()
    from_y(n_dom - 1)
    for step in range(n_y):
        base = lax.rem(sibling + 2 * step, n_panel) * n_dom
        for j in range(n_dom):
            sib_copy(base + j).wait_recv()
            add_norm(base + j)

    def fold(q, value):
        return value if q == 0 else pltpu.roll(value, cols - q * ref_rows, 1)

    scores = jnp.zeros((SHIFTS * rows, cols), F32)
    half_norm = -0.5 * jnp.sum(jnp.transpose(norms[...]), axis=0, keepdims=True)
    half_norm = jnp.broadcast_to(half_norm, (8, cols))
    norm_row = jnp.zeros((8, cols), F32)
    product = lax.dot_general(moved[...], gathered[...], NT, preferred_element_type=F32)
    for q in range(pieces):
        scores += fold(q, product[q * cands:(q + 1) * cands])
        norm_row += fold(q, half_norm)
    column = lax.broadcasted_iota(jnp.int32, (rows, cols), 1)
    valid = (column & (TILE - 1)) < ref_rows
    blocks = []
    for t in range(SHIFTS):
        a, b = offsets(t)
        cost = (a * a + b * b).astype(F32) * PENALTY
        block = scores[t * rows:(t + 1) * rows] + norm_row[:1] - cost
        blocks.append(jnp.where(valid, block, -jnp.inf))
    top = functools.reduce(jnp.maximum, blocks)
    top = jnp.max(top, axis=1, keepdims=True)
    blocks = [jnp.exp(block - top) for block in blocks]
    total = jnp.sum(sum(blocks), axis=1, keepdims=True)
    inverse = 1.0 / total
    weights = jnp.concatenate([(block * inverse).astype(BF16) for block in blocks], axis=0)

    evidence = top + jnp.log(total)
    spot = lax.broadcasted_iota(jnp.int32, (rows, LANES), 0) + panel * rows
    log_row = jnp.sum(jnp.where(lane == spot, evidence, 0.0), axis=0, keepdims=True)
    logs[panel] = jnp.broadcast_to(log_row, (8, LANES))

    def log_copy(step):
        return pltpu.make_async_remote_copy(
            src_ref=logs.at[panel], dst_ref=logs.at[panel], send_sem=log_send.at[step - 1],
            recv_sem=log_recv.at[panel],
            device_id={"panel": lax.rem(panel + step, n_panel)}, device_id_type=MESH,
        )

    for step in range(1, n_panel):
        log_copy(step).start()

    mixed = lax.dot_general(onehot[...], weights, NT, preferred_element_type=F32).astype(BF16)

    chunk = 2 * LANES
    lines = seg_len // LANES
    for c in range(seg_len // chunk):
        total = jnp.zeros((block_total, chunk), F32)
        for s in range(segments):
            q, at = divmod(s * seg_len + c * chunk, width)
            total += jnp.dot(
                mixed[s * block_total:(s + 1) * block_total], moved[q * cands:(q + 1) * cands, at:at + chunk],
                preferred_element_type=F32,
            )
        for k in range(2):
            part32[pl.ds(2 * c + k, block_total, stride=lines), :] = total[:, k * LANES:(k + 1) * LANES]
    part16[...] = part32[...].astype(BF16)

    def tile_of(ref, d):
        return ref.at[pl.ds(pl.multiple_of(d * TILE, TILE), TILE), :]

    def part_copy(d):
        return pltpu.make_async_remote_copy(
            src_ref=tile_of(part16, d), dst_ref=tile_of(landed, me), send_sem=part_send,
            recv_sem=part_recv, device_id=place(d), device_id_type=MESH,
        )

    if n <= 16:
        for far_dom in range(n_dom - 1, -1, -1):
            for far_panel in range(n_panel):
                if far_dom or far_panel:
                    part_copy(
                        lax.rem(panel + far_panel, n_panel) * n_dom + lax.rem(dom + far_dom, n_dom)
                    ).start()
    else:
        @pl.loop(1, n)
        def _(o):
            part_copy(lax.rem(me + o, n)).start()

    own_at = pl.ds(pl.multiple_of(me * TILE, TILE), TILE)
    landed[own_at, :] = jnp.zeros((TILE, LANES), BF16)
    arrivals = pltpu.make_async_remote_copy(
        src_ref=part16.at[:(n - 1) * TILE, :], dst_ref=landed.at[:(n - 1) * TILE, :], send_sem=part_send,
        recv_sem=part_recv, device_id={"panel": sibling}, device_id_type=MESH,
    )
    arrivals.wait_recv()
    total = part32[own_at, :]
    for d in range(n):
        total += landed[d * TILE:(d + 1) * TILE, :].astype(F32)
    total = total * scale
    for k in range(TILE):
        vol_out[k // lines:k // lines + 1, (k % lines) * LANES:(k % lines + 1) * LANES] = total[k:k + 1]

    log_total = logs[panel]
    for step in range(1, n_panel):
        sender = lax.rem(panel + step, n_panel)
        pltpu.make_async_remote_copy(
            src_ref=logs.at[sender], dst_ref=logs.at[sender], send_sem=log_send.at[step - 1],
            recv_sem=log_recv.at[sender], device_id={"panel": sender}, device_id_type=MESH,
        ).wait_recv()
        log_total += logs[sender]
    log_out[...] = log_total[:1, :log_out.shape[1]]

    arrivals.wait_send()

    @pl.when(at_end)
    def _():
        for step in range(1, n_y):
            far_copy(step).wait_send()

    for step in range(1, n_panel):
        slot_copy(step).wait_send()
        log_copy(step).wait_send()
    for j in range(n_dom):
        @pl.when(j != dom)
        def _():
            line_copy(j).wait_send()

        @pl.when(jnp.abs(dom - j) != far)
        def _():
            for step in range(1, n_y):
                y_copy(step, j).wait_send()

        for step in range(n_y):
            sib_copy(y_peer(step) * n_dom + j).wait_send()


def shards(images, shift_index, references, slot_blocks):
    n_panel = lax.axis_size("panel")
    n_dom = lax.axis_size("dom")
    n = n_panel * n_dom
    part_dev, row_width = images.shape
    slot_rows, segments = slot_blocks.shape
    block_total = 2 * n
    volume_scale = (part_dev * n_dom * segments / block_total) ** (-0.5)
    rows = part_dev // n_panel
    width = row_width * references.shape[0] // TILE
    seg_len = row_width // segments
    lines = seg_len // LANES
    vmem = pl.BlockSpec(memory_space=pltpu.VMEM)
    dma = pltpu.SemaphoreType.DMA
    volume, log_evidence = pl.pallas_call(
        functools.partial(kernel, n_panel, n_dom, volume_scale),
        out_shape=(
            jax.ShapeDtypeStruct((2, seg_len), F32),
            jax.ShapeDtypeStruct((1, part_dev), F32),
        ),
        in_specs=[pl.BlockSpec(memory_space=pltpu.HBM)] * 4,
        out_specs=(vmem, vmem),
        scratch_shapes=[
            pltpu.VMEM((rows, row_width), BF16),
            pltpu.VMEM(references.shape, BF16),
            pltpu.VMEM((SHIFTS, part_dev), jnp.int32),
            pltpu.VMEM((TILE, LANES), F32),
            pltpu.VMEM((LANES, TILE), jnp.int32),
            pltpu.VMEM((TILE, width), F32),
            pltpu.VMEM((n * TILE, width), BF16),
            pltpu.VMEM((n * TILE, LANES), F32),
            pltpu.VMEM((SHIFTS * rows * (row_width // width), width), BF16),
            pltpu.VMEM((segments, slot_rows), jnp.int32),
            pltpu.VMEM((n_panel, segments, LANES), jnp.int32),
            pltpu.VMEM((segments * block_total, n * TILE), BF16),
            pltpu.VMEM((block_total * lines, LANES), F32),
            pltpu.VMEM((block_total * lines, LANES), BF16),
            pltpu.VMEM((n * TILE, LANES), BF16),
            pltpu.VMEM((n_panel, 8, LANES), F32),
            dma((4,)),
            dma((n,)),
            dma((n_dom,)),
            dma((max(n_panel // 2 - 1, 1),)),
            dma((max(n_panel // 2 - 1, 1), n_dom)),
            dma((n,)),
            dma((n_panel,)),
            dma((n_panel,)),
            dma(()),
            dma(()),
            dma((n_panel,)),
            dma((n_panel,)),
        ],
        compiler_params=pltpu.CompilerParams(
            collective_id=0, has_side_effects=True, vmem_limit_bytes=56 * 1024 * 1024
        ),
        name="expectation_backprojection",
    )(images, shift_index.T, references, slot_blocks.T)
    return volume, log_evidence.reshape(part_dev)


def solution(mesh):
    in_specs = (
        P(("half", "dom"), None),
        P(("half", "dom"), None),
        P(("half", "panel", "dom"), None),
        P(("half", "panel"), None),
    )
    out_specs = (P(("half", "panel", "dom"), None), P(("half", "dom")))
    return jax.shard_map(shards, mesh=mesh, in_specs=in_specs, out_specs=out_specs, check_vma=False)
```

```python
import functools
import math

import jax
import jax.numpy as jnp
from jax import lax
from jax.experimental import pallas as pl
from jax.experimental.pallas import tpu as pltpu
from jax.sharding import PartitionSpec as P

MESH = pl.DeviceIdType.MESH
PIX = 64
SHIFTS = 9
LANES = 128
TILE = 16
T_GROUP = 3
U_BLOCK = 8
PENALTY = 0.125
F32 = jnp.float32
BF16 = jnp.bfloat16
NT = (((1,), (1,)), ((), ()))


def row_offset(index):
    return (index * 37) >> 8


def kernel(
    n_panel, n_dom, scale, images, shift, refs, slots, vol_out, log_out,
    img, refs_in, shift_in, shift_pad, shift_col, refs32, gathered, norms, moved, slot_in, slot_all, onehot,
    part32, part16, landed, logs, in_sem, recv_sem, z_sem, y_sem, sib_sem, slot_send, slot_recv,
    part_send, part_recv, log_send, log_recv,
):
    n = n_panel * n_dom
    n_y = n_panel // 2
    panel, dom = lax.axis_index("panel"), lax.axis_index("dom")
    me = panel * n_dom + dom
    rows = img.shape[0]
    ref_rows = refs.shape[0]
    pieces = TILE // ref_rows
    width = gathered.shape[1]
    cols = gathered.shape[0]
    cands = SHIFTS * rows
    segments = slots.shape[0]
    seg_len = img.shape[1] // segments
    block_total = 2 * n
    core = lax.rem(panel, 2)
    sibling = panel + 1 - 2 * core

    def y_peer(step):
        return lax.rem(panel + 2 * step, n_panel)

    def place(d):
        return {"panel": lax.div(d, n_dom), "dom": lax.rem(d, n_dom)}

    barrier = pltpu.get_barrier_semaphore()

    @pl.loop(1, n_dom)
    def _(o):
        pl.semaphore_signal(
            barrier, inc=1, device_id={"dom": lax.rem(dom + o, n_dom)}, device_id_type=MESH
        )

    for step in range(1, n_panel):
        pl.semaphore_signal(
            barrier, inc=1, device_id={"panel": lax.rem(panel + step, n_panel)}, device_id_type=MESH
        )

    first = pl.multiple_of(panel * rows, rows)
    refs_copy = pltpu.make_async_copy(refs, refs_in, in_sem.at[0])
    img_copy = pltpu.make_async_copy(images.at[pl.ds(first, rows), :], img, in_sem.at[1])
    shift_copy = pltpu.make_async_copy(shift, shift_in, in_sem.at[2])
    slot_load = pltpu.make_async_copy(slots, slot_in, in_sem.at[3])
    refs_copy.start()
    shift_copy.start()
    slot_load.start()
    img_copy.start()

    def shard(d):
        return gathered.at[pl.ds(pl.multiple_of(d * TILE, TILE), TILE), :]

    def add_norm(d):
        at = pl.ds(pl.multiple_of(d * TILE, TILE), TILE)
        total = jnp.zeros((TILE, LANES), F32)
        for k in range(width // LANES):
            value = gathered[at, k * LANES:(k + 1) * LANES].astype(F32)
            total += value * value
        norms[at, :] = total

    refs_copy.wait()
    for q in range(pieces):
        refs32[q * ref_rows:(q + 1) * ref_rows, :] = refs_in[:, q * width:(q + 1) * width].astype(F32)
    gathered[pl.ds(pl.multiple_of(me * TILE, TILE), TILE), :] = refs32[...].astype(BF16)
    slot_load.wait()
    slot_all[panel] = jnp.zeros((segments, LANES), jnp.int32)
    slot_all[panel, :, :slots.shape[1]] = slot_in[...]

    pl.semaphore_wait(barrier, n_dom + n_panel - 2)

    def shard_copy(d, device, sem):
        return pltpu.make_async_remote_copy(
            src_ref=shard(d), dst_ref=shard(d), send_sem=sem, recv_sem=recv_sem.at[d],
            device_id=device, device_id_type=MESH,
        )

    def line_copy(target):
        return shard_copy(me, {"dom": target}, z_sem.at[target])

    def y_copy(step, j):
        return shard_copy(panel * n_dom + j, {"panel": y_peer(step)}, y_sem.at[step - 1, j])

    def sib_copy(d):
        return shard_copy(d, {"panel": sibling}, sib_sem.at[d])

    def relay(j):
        for step in range(1, n_y):
            y_copy(step, j).start()
        sib_copy(panel * n_dom + j).start()

    def from_line(j):
        sib_copy(panel * n_dom + j).wait_recv()
        relay(j)
        add_norm(panel * n_dom + j)

    def at_distance(s, do):
        pl.when(dom - s >= 0)(lambda: do(dom - s))
        pl.when(dom + s < n_dom)(lambda: do(dom + s))

    def from_y(s):
        for step in range(1, n_y):
            base = y_peer(step) * n_dom

            def pass_on(j):
                sib_copy(base + j).wait_recv()
                sib_copy(base + j).start()
                add_norm(base + j)

            if s > 0:
                at_distance(s, pass_on)
            else:
                pass_on(dom)

    def slot_copy(step):
        own = slot_all.at[panel]
        return pltpu.make_async_remote_copy(
            src_ref=own, dst_ref=own, send_sem=slot_send.at[step - 1], recv_sem=slot_recv.at[panel],
            device_id={"panel": lax.rem(panel + step, n_panel)}, device_id_type=MESH,
        )

    def send_line(s):
        at_distance(s, lambda target: line_copy(target).start())

    late = n_dom - 1 if n_dom > 3 else n_dom
    for s in range(1, late):
        send_line(s)
        if s == 1:
            for step in range(1, n_y):
                y_copy(step, dom).start()
    sib_copy(me).start()
    for step in range(1, n_panel):
        slot_copy(step).start()

    lane = lax.broadcasted_iota(jnp.int32, (rows, LANES), 1)
    turn_sign = jnp.where(lane < PIX, -1.0, 1.0).astype(F32)
    freq_col = (lane & (PIX - 1)) - PIX // 2

    shift_copy.wait()
    shift_pad[...] = jnp.zeros(shift_pad.shape, F32)
    shift_pad[:SHIFTS, :shift.shape[1]] = shift_in[...].astype(F32)
    shift_col[...] = jnp.transpose(shift_pad[...]).astype(jnp.int32)

    multiple = lax.broadcasted_iota(jnp.int32, (8, LANES), 0)
    turns = (freq_col[:8] * multiple + PIX // 2) & (PIX - 1)
    angle = (turns - PIX // 2).astype(F32) * (-2.0 * math.pi / PIX)
    cos_rows, sin_rows = jnp.cos(angle), jnp.sin(angle)

    def offsets(t):
        index = shift_col[pl.ds(first, rows), t:t + 1]
        a = row_offset(index)
        return a - 3, index - 7 * a - 3

    def pick(k, options):
        out = options[0]
        for i in range(1, len(options)):
            out = jnp.where(k == i, options[i], out)
        return out

    blocks_per_piece = width // (U_BLOCK * LANES)

    def shift_group(t0):
        parts = []
        for t in range(t0, t0 + T_GROUP):
            a, b = offsets(t)
            a = jnp.broadcast_to(a, (rows, LANES))
            b = jnp.broadcast_to(b, (rows, LANES))
            flip = jnp.where((a & 1) == 1, -1.0, 1.0).astype(F32)
            far_a, far_b = jnp.abs(a), jnp.abs(b)
            cosine = flip * pick(far_b, [cos_rows[k:k + 1] for k in range(4)])
            sine = flip * pick(far_b, [sin_rows[k:k + 1] for k in range(4)]) * turn_sign
            sine = jnp.where(b < 0, -sine, sine)
            turn_cos = pick(far_a, [jnp.full((rows, LANES), math.cos(2 * math.pi * k / PIX), F32) for k in range(4)])
            turn_sin = pick(far_a, [jnp.full((rows, LANES), math.sin(2 * math.pi * k / PIX), F32) for k in range(4)])
            turn_sin = jnp.where(a < 0, turn_sin, -turn_sin) * turn_sign
            parts.append((cosine, sine, turn_cos, turn_sin))
        cosine, sine, turn_cos, turn_sin = (jnp.concatenate(x, axis=0) for x in zip(*parts))

        def body(block, carry):
            cosine, sine = carry
            q = lax.div(block, blocks_per_piece)
            lane0 = lax.rem(block, blocks_per_piece) * (U_BLOCK * LANES)
            at_rows = pl.ds(pl.multiple_of(q * cands + t0 * rows, rows), T_GROUP * rows)
            for k in range(U_BLOCK):
                at = pl.multiple_of((block * U_BLOCK + k) * LANES, LANES)
                to = pl.multiple_of(lane0 + k * LANES, LANES)
                x = img[:, pl.ds(at, LANES)].astype(F32)
                swapped = pltpu.roll(x, PIX, 1)
                x = jnp.concatenate([x] * T_GROUP, axis=0)
                swapped = jnp.concatenate([swapped] * T_GROUP, axis=0)
                moved[at_rows, pl.ds(to, LANES)] = (x * cosine + swapped * sine).astype(BF16)
                cosine, sine = cosine * turn_cos - sine * turn_sin, sine * turn_cos + cosine * turn_sin
            return cosine, sine

        lax.fori_loop(0, PIX // U_BLOCK, body, (cosine, sine))

    def build_onehot():
        for step in range(1, n_panel):
            sender = lax.rem(panel + step, n_panel)
            pltpu.make_async_remote_copy(
                src_ref=slot_all.at[sender], dst_ref=slot_all.at[sender], send_sem=slot_send.at[step - 1],
                recv_sem=slot_recv.at[sender], device_id={"panel": sender}, device_id_type=MESH,
            ).wait_recv()
        spread_col = lax.broadcasted_iota(jnp.int32, (LANES, cols), 1)
        spread_row = lax.broadcasted_iota(jnp.int32, (LANES, cols), 0)
        within = spread_col & (TILE - 1)
        spread_to = jnp.where(within < ref_rows, (spread_col >> 4) * ref_rows + within, -1)
        slot_of = jnp.zeros((segments, cols), F32)
        for k in range(n_panel):
            spread = jnp.where(spread_row + k * slots.shape[1] == spread_to, 1.0, 0.0)
            spread = jnp.where(spread_row < slots.shape[1], spread, 0.0).astype(BF16)
            slot_of += jnp.dot(slot_all[k].astype(F32).astype(BF16), spread, preferred_element_type=F32)
        block_id = lax.broadcasted_iota(jnp.int32, (block_total, cols), 0).astype(F32)
        for s in range(segments):
            onehot[s * block_total:(s + 1) * block_total, :] = jnp.where(
                block_id == slot_of[s:s + 1], 1.0, 0.0
            ).astype(BF16)

    img_copy.wait()
    for t0 in range(0, SHIFTS, T_GROUP):
        shift_group(t0)
    for s in range(late, n_dom):
        send_line(s)
    add_norm(me)
    for s in range(1, n_dom):
        at_distance(s, from_line)
        from_y(s - 1)
        if s == 1:
            build_onehot()
    if n_dom == 1:
        build_onehot()
    from_y(n_dom - 1)
    for step in range(n_y):
        base = lax.rem(sibling + 2 * step, n_panel) * n_dom
        for j in range(n_dom):
            sib_copy(base + j).wait_recv()
            add_norm(base + j)

    def fold(q, value):
        return value if q == 0 else pltpu.roll(value, cols - q * ref_rows, 1)

    scores = jnp.zeros((SHIFTS * rows, cols), F32)
    half_norm = -0.5 * jnp.sum(jnp.transpose(norms[...]), axis=0, keepdims=True)
    half_norm = jnp.broadcast_to(half_norm, (8, cols))
    norm_row = jnp.zeros((8, cols), F32)
    product = lax.dot_general(moved[...], gathered[...], NT, preferred_element_type=F32)
    for q in range(pieces):
        scores += fold(q, product[q * cands:(q + 1) * cands])
        norm_row += fold(q, half_norm)
    column = lax.broadcasted_iota(jnp.int32, (rows, cols), 1)
    valid = (column & (TILE - 1)) < ref_rows
    blocks = []
    for t in range(SHIFTS):
        a, b = offsets(t)
        cost = (a * a + b * b).astype(F32) * PENALTY
        block = scores[t * rows:(t + 1) * rows] + norm_row[:1] - cost
        blocks.append(jnp.where(valid, block, -jnp.inf))
    top = functools.reduce(jnp.maximum, blocks)
    top = jnp.max(top, axis=1, keepdims=True)
    blocks = [jnp.exp(block - top) for block in blocks]
    total = jnp.sum(sum(blocks), axis=1, keepdims=True)
    inverse = 1.0 / total
    weights = jnp.concatenate([(block * inverse).astype(BF16) for block in blocks], axis=0)

    evidence = top + jnp.log(total)
    spot = lax.broadcasted_iota(jnp.int32, (rows, LANES), 0) + panel * rows
    log_row = jnp.sum(jnp.where(lane == spot, evidence, 0.0), axis=0, keepdims=True)
    logs[panel] = jnp.broadcast_to(log_row, (8, LANES))

    def log_copy(step):
        return pltpu.make_async_remote_copy(
            src_ref=logs.at[panel], dst_ref=logs.at[panel], send_sem=log_send.at[step - 1],
            recv_sem=log_recv.at[panel],
            device_id={"panel": lax.rem(panel + step, n_panel)}, device_id_type=MESH,
        )

    for step in range(1, n_panel):
        log_copy(step).start()

    mixed = lax.dot_general(onehot[...], weights, NT, preferred_element_type=F32).astype(BF16)

    chunk = 2 * LANES
    lines = seg_len // LANES
    for c in range(seg_len // chunk):
        total = jnp.zeros((block_total, chunk), F32)
        for s in range(segments):
            q, at = divmod(s * seg_len + c * chunk, width)
            total += jnp.dot(
                mixed[s * block_total:(s + 1) * block_total], moved[q * cands:(q + 1) * cands, at:at + chunk],
                preferred_element_type=F32,
            )
        for k in range(2):
            part32[pl.ds(2 * c + k, block_total, stride=lines), :] = total[:, k * LANES:(k + 1) * LANES]
    part16[...] = part32[...].astype(BF16)

    def tile_of(ref, d):
        return ref.at[pl.ds(pl.multiple_of(d * TILE, TILE), TILE), :]

    def part_copy(d):
        return pltpu.make_async_remote_copy(
            src_ref=tile_of(part16, d), dst_ref=tile_of(landed, me), send_sem=part_send,
            recv_sem=part_recv, device_id=place(d), device_id_type=MESH,
        )

    if n <= 16:
        for far_dom in range(n_dom - 1, -1, -1):
            for far_panel in range(n_panel):
                if far_dom or far_panel:
                    part_copy(
                        lax.rem(panel + far_panel, n_panel) * n_dom + lax.rem(dom + far_dom, n_dom)
                    ).start()
    else:
        @pl.loop(1, n)
        def _(o):
            part_copy(lax.rem(me + o, n)).start()

    own_at = pl.ds(pl.multiple_of(me * TILE, TILE), TILE)
    landed[own_at, :] = jnp.zeros((TILE, LANES), BF16)
    arrivals = pltpu.make_async_remote_copy(
        src_ref=part16.at[:(n - 1) * TILE, :], dst_ref=landed.at[:(n - 1) * TILE, :], send_sem=part_send,
        recv_sem=part_recv, device_id={"panel": sibling}, device_id_type=MESH,
    )
    arrivals.wait_recv()
    total = part32[own_at, :]
    for d in range(n):
        total += landed[d * TILE:(d + 1) * TILE, :].astype(F32)
    total = total * scale
    for k in range(TILE):
        vol_out[k // lines:k // lines + 1, (k % lines) * LANES:(k % lines + 1) * LANES] = total[k:k + 1]

    log_total = logs[panel]
    for step in range(1, n_panel):
        sender = lax.rem(panel + step, n_panel)
        pltpu.make_async_remote_copy(
            src_ref=logs.at[sender], dst_ref=logs.at[sender], send_sem=log_send.at[step - 1],
            recv_sem=log_recv.at[sender], device_id={"panel": sender}, device_id_type=MESH,
        ).wait_recv()
        log_total += logs[sender]
    log_out[...] = log_total[:1, :log_out.shape[1]]

    arrivals.wait_send()

    for step in range(1, n_panel):
        slot_copy(step).wait_send()
        log_copy(step).wait_send()
    for j in range(n_dom):
        @pl.when(j != dom)
        def _():
            line_copy(j).wait_send()

        for step in range(1, n_y):
            y_copy(step, j).wait_send()
        for step in range(n_y):
            sib_copy(y_peer(step) * n_dom + j).wait_send()


def shards(images, shift_index, references, slot_blocks):
    n_panel = lax.axis_size("panel")
    n_dom = lax.axis_size("dom")
    n = n_panel * n_dom
    part_dev, row_width = images.shape
    slot_rows, segments = slot_blocks.shape
    block_total = 2 * n
    volume_scale = (part_dev * n_dom * segments / block_total) ** (-0.5)
    rows = part_dev // n_panel
    width = row_width * references.shape[0] // TILE
    seg_len = row_width // segments
    lines = seg_len // LANES
    vmem = pl.BlockSpec(memory_space=pltpu.VMEM)
    dma = pltpu.SemaphoreType.DMA
    volume, log_evidence = pl.pallas_call(
        functools.partial(kernel, n_panel, n_dom, volume_scale),
        out_shape=(
            jax.ShapeDtypeStruct((2, seg_len), F32),
            jax.ShapeDtypeStruct((1, part_dev), F32),
        ),
        in_specs=[pl.BlockSpec(memory_space=pltpu.HBM)] * 4,
        out_specs=(vmem, vmem),
        scratch_shapes=[
            pltpu.VMEM((rows, row_width), BF16),
            pltpu.VMEM(references.shape, BF16),
            pltpu.VMEM((SHIFTS, part_dev), jnp.int32),
            pltpu.VMEM((TILE, LANES), F32),
            pltpu.VMEM((LANES, TILE), jnp.int32),
            pltpu.VMEM((TILE, width), F32),
            pltpu.VMEM((n * TILE, width), BF16),
            pltpu.VMEM((n * TILE, LANES), F32),
            pltpu.VMEM((SHIFTS * rows * (row_width // width), width), BF16),
            pltpu.VMEM((segments, slot_rows), jnp.int32),
            pltpu.VMEM((n_panel, segments, LANES), jnp.int32),
            pltpu.VMEM((segments * block_total, n * TILE), BF16),
            pltpu.VMEM((block_total * lines, LANES), F32),
            pltpu.VMEM((block_total * lines, LANES), BF16),
            pltpu.VMEM((n * TILE, LANES), BF16),
            pltpu.VMEM((n_panel, 8, LANES), F32),
            dma((4,)),
            dma((n,)),
            dma((n_dom,)),
            dma((max(n_panel // 2 - 1, 1), n_dom)),
            dma((n,)),
            dma((n_panel,)),
            dma((n_panel,)),
            dma(()),
            dma(()),
            dma((n_panel,)),
            dma((n_panel,)),
        ],
        compiler_params=pltpu.CompilerParams(
            collective_id=0, has_side_effects=True, vmem_limit_bytes=56 * 1024 * 1024
        ),
        name="expectation_backprojection",
    )(images, shift_index.T, references, slot_blocks.T)
    return volume, log_evidence.reshape(part_dev)


def solution(mesh):
    in_specs = (
        P(("half", "dom"), None),
        P(("half", "dom"), None),
        P(("half", "panel", "dom"), None),
        P(("half", "panel"), None),
    )
    out_specs = (P(("half", "panel", "dom"), None), P(("half", "dom")))
    return jax.shard_map(shards, mesh=mesh, in_specs=in_specs, out_specs=out_specs, check_vma=False)
```

```python
import functools
import math

import jax
import jax.numpy as jnp
from jax import lax
from jax.experimental import pallas as pl
from jax.experimental.pallas import tpu as pltpu
from jax.sharding import PartitionSpec as P

MESH = pl.DeviceIdType.MESH
PIX = 64
SHIFTS = 9
LANES = 128
TILE = 16
T_GROUP = 3
U_BLOCK = 8
PENALTY = 0.125
F32 = jnp.float32
BF16 = jnp.bfloat16
NT = (((1,), (1,)), ((), ()))


def row_offset(index):
    return (index * 37) >> 8


def kernel(
    n_panel, n_dom, scale, images, shift, refs, slots, vol_out, log_out,
    img, refs_in, shift_in, shift_pad, shift_col, refs32, gathered, norms, moved, slot_in, slot_all, onehot,
    part32, part16, landed, logs, in_sem, recv_sem, z_sem, y_sem, sib_sem, slot_send, slot_recv,
    part_send, part_recv, log_send, log_recv,
):
    n = n_panel * n_dom
    n_y = n_panel // 2
    panel, dom = lax.axis_index("panel"), lax.axis_index("dom")
    me = panel * n_dom + dom
    rows = img.shape[0]
    ref_rows = refs.shape[0]
    pieces = TILE // ref_rows
    width = gathered.shape[1]
    cols = gathered.shape[0]
    cands = SHIFTS * rows
    segments = slots.shape[0]
    seg_len = img.shape[1] // segments
    block_total = 2 * n
    core = lax.rem(panel, 2)
    sibling = panel + 1 - 2 * core

    def y_peer(step):
        return lax.rem(panel + 2 * step, n_panel)

    def place(d):
        return {"panel": lax.div(d, n_dom), "dom": lax.rem(d, n_dom)}

    barrier = pltpu.get_barrier_semaphore()

    @pl.loop(1, n_dom)
    def _(o):
        pl.semaphore_signal(
            barrier, inc=1, device_id={"dom": lax.rem(dom + o, n_dom)}, device_id_type=MESH
        )

    for step in range(1, n_panel):
        pl.semaphore_signal(
            barrier, inc=1, device_id={"panel": lax.rem(panel + step, n_panel)}, device_id_type=MESH
        )

    first = pl.multiple_of(panel * rows, rows)
    refs_copy = pltpu.make_async_copy(refs, refs_in, in_sem.at[0])
    img_copy = pltpu.make_async_copy(images.at[pl.ds(first, rows), :], img, in_sem.at[1])
    shift_copy = pltpu.make_async_copy(shift, shift_in, in_sem.at[2])
    slot_load = pltpu.make_async_copy(slots, slot_in, in_sem.at[3])
    refs_copy.start()
    shift_copy.start()
    slot_load.start()
    img_copy.start()

    def shard(d):
        return gathered.at[pl.ds(pl.multiple_of(d * TILE, TILE), TILE), :]

    def add_norm(d):
        at = pl.ds(pl.multiple_of(d * TILE, TILE), TILE)
        total = jnp.zeros((TILE, LANES), F32)
        for k in range(width // LANES):
            value = gathered[at, k * LANES:(k + 1) * LANES].astype(F32)
            total += value * value
        norms[at, :] = total

    refs_copy.wait()
    for q in range(pieces):
        refs32[q * ref_rows:(q + 1) * ref_rows, :] = refs_in[:, q * width:(q + 1) * width].astype(F32)
    gathered[pl.ds(pl.multiple_of(me * TILE, TILE), TILE), :] = refs32[...].astype(BF16)
    slot_load.wait()
    slot_all[panel] = jnp.zeros((segments, LANES), jnp.int32)
    slot_all[panel, :, :slots.shape[1]] = slot_in[...]

    pl.semaphore_wait(barrier, n_dom + n_panel - 2)

    def shard_copy(d, device, sem):
        return pltpu.make_async_remote_copy(
            src_ref=shard(d), dst_ref=shard(d), send_sem=sem, recv_sem=recv_sem.at[d],
            device_id=device, device_id_type=MESH,
        )

    def line_copy(target):
        return shard_copy(me, {"dom": target}, z_sem.at[target])

    def y_copy(step, j):
        return shard_copy(panel * n_dom + j, {"panel": y_peer(step)}, y_sem.at[step - 1, j])

    def sib_copy(d):
        return shard_copy(d, {"panel": sibling}, sib_sem.at[d])

    def relay(j):
        for step in range(1, n_y):
            y_copy(step, j).start()
        sib_copy(panel * n_dom + j).start()

    def from_line(j):
        sib_copy(panel * n_dom + j).wait_recv()
        relay(j)
        add_norm(panel * n_dom + j)

    def at_distance(s, do):
        pl.when(dom - s >= 0)(lambda: do(dom - s))
        pl.when(dom + s < n_dom)(lambda: do(dom + s))

    def from_y(s):
        for step in range(1, n_y):
            base = y_peer(step) * n_dom

            def pass_on(j):
                sib_copy(base + j).wait_recv()
                sib_copy(base + j).start()
                add_norm(base + j)

            if s > 0:
                at_distance(s, pass_on)
            else:
                pass_on(dom)

    def slot_copy(step):
        own = slot_all.at[panel]
        return pltpu.make_async_remote_copy(
            src_ref=own, dst_ref=own, send_sem=slot_send.at[step - 1], recv_sem=slot_recv.at[panel],
            device_id={"panel": lax.rem(panel + step, n_panel)}, device_id_type=MESH,
        )

    def send_line(s):
        at_distance(s, lambda target: line_copy(target).start())

    late = n_dom - 1 if n_dom > 3 else n_dom
    for s in range(1, late):
        send_line(s)
        if s == 1:
            for step in range(1, n_y):
                y_copy(step, dom).start()
    sib_copy(me).start()
    for step in range(1, n_panel):
        slot_copy(step).start()

    lane = lax.broadcasted_iota(jnp.int32, (rows, LANES), 1)
    turn_sign = jnp.where(lane < PIX, -1.0, 1.0).astype(F32)
    freq_col = (lane & (PIX - 1)) - PIX // 2

    shift_copy.wait()
    shift_pad[...] = jnp.zeros(shift_pad.shape, F32)
    shift_pad[:SHIFTS, :shift.shape[1]] = shift_in[...].astype(F32)
    shift_col[...] = jnp.transpose(shift_pad[...]).astype(jnp.int32)

    multiple = lax.broadcasted_iota(jnp.int32, (8, LANES), 0)
    turns = (freq_col[:8] * multiple + PIX // 2) & (PIX - 1)
    angle = (turns - PIX // 2).astype(F32) * (-2.0 * math.pi / PIX)
    cos_rows, sin_rows = jnp.cos(angle), jnp.sin(angle)

    def offsets(t):
        index = shift_col[pl.ds(first, rows), t:t + 1]
        a = row_offset(index)
        return a - 3, index - 7 * a - 3

    def pick(k, options):
        out = options[0]
        for i in range(1, len(options)):
            out = jnp.where(k == i, options[i], out)
        return out

    blocks_per_piece = width // (U_BLOCK * LANES)

    def shift_group(t0):
        parts = []
        for t in range(t0, t0 + T_GROUP):
            a, b = offsets(t)
            a = jnp.broadcast_to(a, (rows, LANES))
            b = jnp.broadcast_to(b, (rows, LANES))
            flip = jnp.where((a & 1) == 1, -1.0, 1.0).astype(F32)
            far_a, far_b = jnp.abs(a), jnp.abs(b)
            cosine = flip * pick(far_b, [cos_rows[k:k + 1] for k in range(4)])
            sine = flip * pick(far_b, [sin_rows[k:k + 1] for k in range(4)]) * turn_sign
            sine = jnp.where(b < 0, -sine, sine)
            turn_cos = pick(far_a, [jnp.full((rows, LANES), math.cos(2 * math.pi * k / PIX), F32) for k in range(4)])
            turn_sin = pick(far_a, [jnp.full((rows, LANES), math.sin(2 * math.pi * k / PIX), F32) for k in range(4)])
            turn_sin = jnp.where(a < 0, turn_sin, -turn_sin) * turn_sign
            parts.append((cosine, sine, turn_cos, turn_sin))
        cosine, sine, turn_cos, turn_sin = (jnp.concatenate(x, axis=0) for x in zip(*parts))

        def body(block, carry):
            cosine, sine = carry
            q = lax.div(block, blocks_per_piece)
            lane0 = lax.rem(block, blocks_per_piece) * (U_BLOCK * LANES)
            at_rows = pl.ds(pl.multiple_of(q * cands + t0 * rows, rows), T_GROUP * rows)
            for k in range(U_BLOCK):
                at = pl.multiple_of((block * U_BLOCK + k) * LANES, LANES)
                to = pl.multiple_of(lane0 + k * LANES, LANES)
                x = img[:, pl.ds(at, LANES)].astype(F32)
                swapped = pltpu.roll(x, PIX, 1)
                x = jnp.concatenate([x] * T_GROUP, axis=0)
                swapped = jnp.concatenate([swapped] * T_GROUP, axis=0)
                moved[at_rows, pl.ds(to, LANES)] = (x * cosine + swapped * sine).astype(BF16)
                cosine, sine = cosine * turn_cos - sine * turn_sin, sine * turn_cos + cosine * turn_sin
            return cosine, sine

        lax.fori_loop(0, PIX // U_BLOCK, body, (cosine, sine))

    def build_onehot():
        for step in range(1, n_panel):
            sender = lax.rem(panel + step, n_panel)
            pltpu.make_async_remote_copy(
                src_ref=slot_all.at[sender], dst_ref=slot_all.at[sender], send_sem=slot_send.at[step - 1],
                recv_sem=slot_recv.at[sender], device_id={"panel": sender}, device_id_type=MESH,
            ).wait_recv()
        spread_col = lax.broadcasted_iota(jnp.int32, (LANES, cols), 1)
        spread_row = lax.broadcasted_iota(jnp.int32, (LANES, cols), 0)
        within = spread_col & (TILE - 1)
        spread_to = jnp.where(within < ref_rows, (spread_col >> 4) * ref_rows + within, -1)
        slot_of = jnp.zeros((segments, cols), F32)
        for k in range(n_panel):
            spread = jnp.where(spread_row + k * slots.shape[1] == spread_to, 1.0, 0.0)
            spread = jnp.where(spread_row < slots.shape[1], spread, 0.0).astype(BF16)
            slot_of += jnp.dot(slot_all[k].astype(F32).astype(BF16), spread, preferred_element_type=F32)
        block_id = lax.broadcasted_iota(jnp.int32, (block_total, cols), 0).astype(F32)
        for s in range(segments):
            onehot[s * block_total:(s + 1) * block_total, :] = jnp.where(
                block_id == slot_of[s:s + 1], 1.0, 0.0
            ).astype(BF16)

    img_copy.wait()
    for t0 in range(0, SHIFTS, T_GROUP):
        shift_group(t0)
    for s in range(late, n_dom):
        send_line(s)
    add_norm(me)
    for s in range(1, n_dom):
        at_distance(s, from_line)
        from_y(s - 1)
        if s == 1:
            build_onehot()
    if n_dom == 1:
        build_onehot()
    from_y(n_dom - 1)
    for step in range(n_y):
        base = lax.rem(sibling + 2 * step, n_panel) * n_dom
        for j in range(n_dom):
            sib_copy(base + j).wait_recv()
            add_norm(base + j)

    def fold(q, value):
        return value if q == 0 else pltpu.roll(value, cols - q * ref_rows, 1)

    scores = jnp.zeros((SHIFTS * rows, cols), F32)
    half_norm = -0.5 * jnp.sum(jnp.transpose(norms[...]), axis=0, keepdims=True)
    half_norm = jnp.broadcast_to(half_norm, (8, cols))
    norm_row = jnp.zeros((8, cols), F32)
    product = lax.dot_general(moved[...], gathered[...], NT, preferred_element_type=F32)
    for q in range(pieces):
        scores += fold(q, product[q * cands:(q + 1) * cands])
        norm_row += fold(q, half_norm)
    column = lax.broadcasted_iota(jnp.int32, (rows, cols), 1)
    valid = (column & (TILE - 1)) < ref_rows
    blocks = []
    for t in range(SHIFTS):
        a, b = offsets(t)
        cost = (a * a + b * b).astype(F32) * PENALTY
        block = scores[t * rows:(t + 1) * rows] + norm_row[:1] - cost
        blocks.append(jnp.where(valid, block, -jnp.inf))
    top = functools.reduce(jnp.maximum, blocks)
    top = jnp.max(top, axis=1, keepdims=True)
    blocks = [jnp.exp(block - top) for block in blocks]
    total = jnp.sum(sum(blocks), axis=1, keepdims=True)
    inverse = 1.0 / total
    weights = jnp.concatenate([(block * inverse).astype(BF16) for block in blocks], axis=0)

    evidence = top + jnp.log(total)
    spot = lax.broadcasted_iota(jnp.int32, (rows, LANES), 0) + panel * rows
    log_row = jnp.sum(jnp.where(lane == spot, evidence, 0.0), axis=0, keepdims=True)
    logs[panel] = jnp.broadcast_to(log_row, (8, LANES))

    def log_copy(step):
        return pltpu.make_async_remote_copy(
            src_ref=logs.at[panel], dst_ref=logs.at[panel], send_sem=log_send.at[step - 1],
            recv_sem=log_recv.at[panel],
            device_id={"panel": lax.rem(panel + step, n_panel)}, device_id_type=MESH,
        )

    for step in range(1, n_panel):
        log_copy(step).start()

    mixed = lax.dot_general(onehot[...], weights, NT, preferred_element_type=F32).astype(BF16)

    chunk = 2 * LANES
    lines = seg_len // LANES
    for c in range(seg_len // chunk):
        total = jnp.zeros((block_total, chunk), F32)
        for s in range(segments):
            q, at = divmod(s * seg_len + c * chunk, width)
            total += jnp.dot(
                mixed[s * block_total:(s + 1) * block_total], moved[q * cands:(q + 1) * cands, at:at + chunk],
                preferred_element_type=F32,
            )
        for k in range(2):
            part32[pl.ds(2 * c + k, block_total, stride=lines), :] = total[:, k * LANES:(k + 1) * LANES]
    part16[...] = part32[...].astype(BF16)

    def tile_of(ref, d):
        return ref.at[pl.ds(pl.multiple_of(d * TILE, TILE), TILE), :]

    def part_copy(d):
        return pltpu.make_async_remote_copy(
            src_ref=tile_of(part16, d), dst_ref=tile_of(landed, me), send_sem=part_send,
            recv_sem=part_recv, device_id=place(d), device_id_type=MESH,
        )

    if n <= 16:
        for far_dom in range(n_dom - 1, -1, -1):
            for far_panel in range(n_panel):
                if far_dom or far_panel:
                    part_copy(
                        lax.rem(panel + far_panel, n_panel) * n_dom + lax.rem(dom + far_dom, n_dom)
                    ).start()
    else:
        @pl.loop(1, n)
        def _(o):
            part_copy(lax.rem(me + o, n)).start()

    own_at = pl.ds(pl.multiple_of(me * TILE, TILE), TILE)
    landed[own_at, :] = jnp.zeros((TILE, LANES), BF16)
    arrivals = pltpu.make_async_remote_copy(
        src_ref=part16.at[:(n - 1) * TILE, :], dst_ref=landed.at[:(n - 1) * TILE, :], send_sem=part_send,
        recv_sem=part_recv, device_id={"panel": sibling}, device_id_type=MESH,
    )
    arrivals.wait_recv()
    total = part32[own_at, :]
    for d in range(n):
        total += landed[d * TILE:(d + 1) * TILE, :].astype(F32)
    total = total * scale
    for k in range(TILE):
        vol_out[k // lines:k // lines + 1, (k % lines) * LANES:(k % lines + 1) * LANES] = total[k:k + 1]

    log_total = logs[panel]
    for step in range(1, n_panel):
        sender = lax.rem(panel + step, n_panel)
        pltpu.make_async_remote_copy(
            src_ref=logs.at[sender], dst_ref=logs.at[sender], send_sem=log_send.at[step - 1],
            recv_sem=log_recv.at[sender], device_id={"panel": sender}, device_id_type=MESH,
        ).wait_recv()
        log_total += logs[sender]
    log_out[...] = log_total[:1, :log_out.shape[1]]

    arrivals.wait_send()

    for step in range(1, n_panel):
        slot_copy(step).wait_send()
        log_copy(step).wait_send()
    for j in range(n_dom):
        @pl.when(j != dom)
        def _():
            line_copy(j).wait_send()

        for step in range(1, n_y):
            y_copy(step, j).wait_send()
        for step in range(n_y):
            sib_copy(y_peer(step) * n_dom + j).wait_send()


def shards(images, shift_index, references, slot_blocks):
    n_panel = lax.axis_size("panel")
    n_dom = lax.axis_size("dom")
    n = n_panel * n_dom
    part_dev, row_width = images.shape
    slot_rows, segments = slot_blocks.shape
    block_total = 2 * n
    volume_scale = (part_dev * n_dom * segments / block_total) ** (-0.5)
    rows = part_dev // n_panel
    width = row_width * references.shape[0] // TILE
    seg_len = row_width // segments
    lines = seg_len // LANES
    vmem = pl.BlockSpec(memory_space=pltpu.VMEM)
    dma = pltpu.SemaphoreType.DMA
    volume, log_evidence = pl.pallas_call(
        functools.partial(kernel, n_panel, n_dom, volume_scale),
        out_shape=(
            jax.ShapeDtypeStruct((2, seg_len), F32),
            jax.ShapeDtypeStruct((1, part_dev), F32),
        ),
        in_specs=[pl.BlockSpec(memory_space=pltpu.HBM)] * 4,
        out_specs=(vmem, vmem),
        scratch_shapes=[
            pltpu.VMEM((rows, row_width), BF16),
            pltpu.VMEM(references.shape, BF16),
            pltpu.VMEM((SHIFTS, part_dev), jnp.int32),
            pltpu.VMEM((TILE, LANES), F32),
            pltpu.VMEM((LANES, TILE), jnp.int32),
            pltpu.VMEM((TILE, width), F32),
            pltpu.VMEM((n * TILE, width), BF16),
            pltpu.VMEM((n * TILE, LANES), F32),
            pltpu.VMEM((SHIFTS * rows * (row_width // width), width), BF16),
            pltpu.VMEM((segments, slot_rows), jnp.int32),
            pltpu.VMEM((n_panel, segments, LANES), jnp.int32),
            pltpu.VMEM((segments * block_total, n * TILE), BF16),
            pltpu.VMEM((block_total * lines, LANES), F32),
            pltpu.VMEM((block_total * lines, LANES), BF16),
            pltpu.VMEM((n * TILE, LANES), BF16),
            pltpu.VMEM((n_panel, 8, LANES), F32),
            dma((4,)),
            dma((n,)),
            dma((n_dom,)),
            dma((max(n_panel // 2 - 1, 1), n_dom)),
            dma((n,)),
            dma((n_panel,)),
            dma((n_panel,)),
            dma(()),
            dma(()),
            dma((n_panel,)),
            dma((n_panel,)),
        ],
        compiler_params=pltpu.CompilerParams(
            collective_id=0, has_side_effects=True, vmem_limit_bytes=53 * 1024 * 1024
        ),
        name="expectation_backprojection",
    )(images, shift_index.T, references, slot_blocks.T)
    return volume, log_evidence.reshape(part_dev)


def solution(mesh):
    in_specs = (
        P(("half", "dom"), None),
        P(("half", "dom"), None),
        P(("half", "panel", "dom"), None),
        P(("half", "panel"), None),
    )
    out_specs = (P(("half", "panel", "dom"), None), P(("half", "dom")))
    return jax.shard_map(shards, mesh=mesh, in_specs=in_specs, out_specs=out_specs, check_vma=False)
```

```python
import functools
import math

import jax
import jax.numpy as jnp
from jax import lax
from jax.experimental import pallas as pl
from jax.experimental.pallas import tpu as pltpu
from jax.sharding import PartitionSpec as P

MESH = pl.DeviceIdType.MESH
PIX = 64
SHIFTS = 9
LANES = 128
TILE = 16
T_GROUP = 3
U_BLOCK = 8
PENALTY = 0.125
F32 = jnp.float32
BF16 = jnp.bfloat16
NT = (((1,), (1,)), ((), ()))


def row_offset(index):
    return (index * 37) >> 8


def kernel(
    n_panel, n_dom, scale, images, shift, refs, slots, vol_out, log_out,
    img, refs_in, shift_in, shift_pad, shift_col, refs32, gathered, norms, moved, slot_in, slot_all, onehot,
    part32, part16, landed, logs, in_sem, recv_sem, z_sem, y_sem, sib_sem, slot_send, slot_recv,
    part_send, part_recv, log_send, log_recv,
):
    n = n_panel * n_dom
    n_y = n_panel // 2
    panel, dom = lax.axis_index("panel"), lax.axis_index("dom")
    me = panel * n_dom + dom
    rows = img.shape[0]
    ref_rows = refs.shape[0]
    pieces = TILE // ref_rows
    width = gathered.shape[1]
    cols = gathered.shape[0]
    cands = SHIFTS * rows
    segments = slots.shape[0]
    seg_len = img.shape[1] // segments
    block_total = 2 * n
    core = lax.rem(panel, 2)
    sibling = panel + 1 - 2 * core

    def y_peer(step):
        return lax.rem(panel + 2 * step, n_panel)

    def place(d):
        return {"panel": lax.div(d, n_dom), "dom": lax.rem(d, n_dom)}

    barrier = pltpu.get_barrier_semaphore()

    @pl.loop(1, n_dom)
    def _(o):
        pl.semaphore_signal(
            barrier, inc=1, device_id={"dom": lax.rem(dom + o, n_dom)}, device_id_type=MESH
        )

    for step in range(1, n_panel):
        pl.semaphore_signal(
            barrier, inc=1, device_id={"panel": lax.rem(panel + step, n_panel)}, device_id_type=MESH
        )

    first = pl.multiple_of(panel * rows, rows)
    refs_copy = pltpu.make_async_copy(refs, refs_in, in_sem.at[0])
    img_copy = pltpu.make_async_copy(images.at[pl.ds(first, rows), :], img, in_sem.at[1])
    shift_copy = pltpu.make_async_copy(shift, shift_in, in_sem.at[2])
    slot_load = pltpu.make_async_copy(slots, slot_in, in_sem.at[3])
    refs_copy.start()
    shift_copy.start()
    slot_load.start()
    img_copy.start()

    def shard(d):
        return gathered.at[pl.ds(pl.multiple_of(d * TILE, TILE), TILE), :]

    def add_norm(d):
        at = pl.ds(pl.multiple_of(d * TILE, TILE), TILE)
        total = jnp.zeros((TILE, LANES), F32)
        for k in range(width // LANES):
            value = gathered[at, k * LANES:(k + 1) * LANES].astype(F32)
            total += value * value
        norms[at, :] = total

    refs_copy.wait()
    for q in range(pieces):
        refs32[q * ref_rows:(q + 1) * ref_rows, :] = refs_in[:, q * width:(q + 1) * width].astype(F32)
    gathered[pl.ds(pl.multiple_of(me * TILE, TILE), TILE), :] = refs32[...].astype(BF16)
    slot_load.wait()
    slot_all[panel] = jnp.zeros((segments, LANES), jnp.int32)
    slot_all[panel, :, :slots.shape[1]] = slot_in[...]

    pl.semaphore_wait(barrier, n_dom + n_panel - 2)

    def shard_copy(d, device, sem):
        return pltpu.make_async_remote_copy(
            src_ref=shard(d), dst_ref=shard(d), send_sem=sem, recv_sem=recv_sem.at[d],
            device_id=device, device_id_type=MESH,
        )

    def line_copy(target):
        return shard_copy(me, {"dom": target}, z_sem.at[target])

    def y_copy(step, j):
        return shard_copy(panel * n_dom + j, {"panel": y_peer(step)}, y_sem.at[step - 1, j])

    def sib_copy(d):
        return shard_copy(d, {"panel": sibling}, sib_sem.at[d])

    def relay(j):
        for step in range(1, n_y):
            y_copy(step, j).start()
        sib_copy(panel * n_dom + j).start()

    def from_line(j):
        sib_copy(panel * n_dom + j).wait_recv()
        relay(j)
        add_norm(panel * n_dom + j)

    def at_distance(s, do):
        pl.when(dom - s >= 0)(lambda: do(dom - s))
        pl.when(dom + s < n_dom)(lambda: do(dom + s))

    def from_y(s):
        for step in range(1, n_y):
            base = y_peer(step) * n_dom

            def pass_on(j):
                sib_copy(base + j).wait_recv()
                sib_copy(base + j).start()
                add_norm(base + j)

            if s > 0:
                at_distance(s, pass_on)
            else:
                pass_on(dom)

    def slot_copy(step):
        own = slot_all.at[panel]
        return pltpu.make_async_remote_copy(
            src_ref=own, dst_ref=own, send_sem=slot_send.at[step - 1], recv_sem=slot_recv.at[panel],
            device_id={"panel": lax.rem(panel + step, n_panel)}, device_id_type=MESH,
        )

    def send_line(s):
        at_distance(s, lambda target: line_copy(target).start())

    late = n_dom - 1 if n_dom > 3 else n_dom
    for s in range(1, late):
        send_line(s)
        if s == 1:
            for step in range(1, n_y):
                y_copy(step, dom).start()
    sib_copy(me).start()
    for step in range(1, n_panel):
        slot_copy(step).start()

    lane = lax.broadcasted_iota(jnp.int32, (rows, LANES), 1)
    turn_sign = jnp.where(lane < PIX, -1.0, 1.0).astype(F32)
    freq_col = (lane & (PIX - 1)) - PIX // 2

    shift_copy.wait()
    shift_pad[...] = jnp.zeros(shift_pad.shape, F32)
    shift_pad[:SHIFTS, :shift.shape[1]] = shift_in[...].astype(F32)
    shift_col[...] = jnp.transpose(shift_pad[...]).astype(jnp.int32)

    multiple = lax.broadcasted_iota(jnp.int32, (8, LANES), 0)
    turns = (freq_col[:8] * multiple + PIX // 2) & (PIX - 1)
    angle = (turns - PIX // 2).astype(F32) * (-2.0 * math.pi / PIX)
    cos_rows, sin_rows = jnp.cos(angle), jnp.sin(angle)

    def offsets(t):
        index = shift_col[pl.ds(first, rows), t:t + 1]
        a = row_offset(index)
        return a - 3, index - 7 * a - 3

    def pick(k, options):
        out = options[0]
        for i in range(1, len(options)):
            out = jnp.where(k == i, options[i], out)
        return out

    blocks_per_piece = width // (U_BLOCK * LANES)

    def shift_group(t0):
        parts = []
        for t in range(t0, t0 + T_GROUP):
            a, b = offsets(t)
            a = jnp.broadcast_to(a, (rows, LANES))
            b = jnp.broadcast_to(b, (rows, LANES))
            flip = jnp.where((a & 1) == 1, -1.0, 1.0).astype(F32)
            far_a, far_b = jnp.abs(a), jnp.abs(b)
            cosine = flip * pick(far_b, [cos_rows[k:k + 1] for k in range(4)])
            sine = flip * pick(far_b, [sin_rows[k:k + 1] for k in range(4)]) * turn_sign
            sine = jnp.where(b < 0, -sine, sine)
            turn_cos = pick(far_a, [jnp.full((rows, LANES), math.cos(2 * math.pi * k / PIX), F32) for k in range(4)])
            turn_sin = pick(far_a, [jnp.full((rows, LANES), math.sin(2 * math.pi * k / PIX), F32) for k in range(4)])
            turn_sin = jnp.where(a < 0, turn_sin, -turn_sin) * turn_sign
            parts.append((cosine, sine, turn_cos, turn_sin))
        cosine, sine, turn_cos, turn_sin = (jnp.concatenate(x, axis=0) for x in zip(*parts))

        def body(block, carry):
            cosine, sine = carry
            q = lax.div(block, blocks_per_piece)
            lane0 = lax.rem(block, blocks_per_piece) * (U_BLOCK * LANES)
            at_rows = pl.ds(pl.multiple_of(q * cands + t0 * rows, rows), T_GROUP * rows)
            for k in range(U_BLOCK):
                at = pl.multiple_of((block * U_BLOCK + k) * LANES, LANES)
                to = pl.multiple_of(lane0 + k * LANES, LANES)
                x = img[:, pl.ds(at, LANES)].astype(F32)
                swapped = pltpu.roll(x, PIX, 1)
                x = jnp.concatenate([x] * T_GROUP, axis=0)
                swapped = jnp.concatenate([swapped] * T_GROUP, axis=0)
                moved[at_rows, pl.ds(to, LANES)] = (x * cosine + swapped * sine).astype(BF16)
                cosine, sine = cosine * turn_cos - sine * turn_sin, sine * turn_cos + cosine * turn_sin
            return cosine, sine

        lax.fori_loop(0, PIX // U_BLOCK, body, (cosine, sine))

    def build_onehot():
        for step in range(1, n_panel):
            sender = lax.rem(panel + step, n_panel)
            pltpu.make_async_remote_copy(
                src_ref=slot_all.at[sender], dst_ref=slot_all.at[sender], send_sem=slot_send.at[step - 1],
                recv_sem=slot_recv.at[sender], device_id={"panel": sender}, device_id_type=MESH,
            ).wait_recv()
        spread_col = lax.broadcasted_iota(jnp.int32, (LANES, cols), 1)
        spread_row = lax.broadcasted_iota(jnp.int32, (LANES, cols), 0)
        within = spread_col & (TILE - 1)
        spread_to = jnp.where(within < ref_rows, (spread_col >> 4) * ref_rows + within, -1)
        slot_of = jnp.zeros((segments, cols), F32)
        for k in range(n_panel):
            spread = jnp.where(spread_row + k * slots.shape[1] == spread_to, 1.0, 0.0)
            spread = jnp.where(spread_row < slots.shape[1], spread, 0.0).astype(BF16)
            slot_of += jnp.dot(slot_all[k].astype(F32).astype(BF16), spread, preferred_element_type=F32)
        block_id = lax.broadcasted_iota(jnp.int32, (block_total, cols), 0).astype(F32)
        for s in range(segments):
            onehot[s * block_total:(s + 1) * block_total, :] = jnp.where(
                block_id == slot_of[s:s + 1], 1.0, 0.0
            ).astype(BF16)

    img_copy.wait()
    for t0 in range(0, SHIFTS, T_GROUP):
        shift_group(t0)
    for s in range(late, n_dom):
        send_line(s)
    add_norm(me)
    for s in range(1, n_dom):
        at_distance(s, from_line)
    build_onehot()
    for s in range(n_dom):
        from_y(s)
    for step in range(n_y):
        base = lax.rem(sibling + 2 * step, n_panel) * n_dom
        for j in range(n_dom):
            sib_copy(base + j).wait_recv()
            add_norm(base + j)

    def fold(q, value):
        return value if q == 0 else pltpu.roll(value, cols - q * ref_rows, 1)

    scores = jnp.zeros((SHIFTS * rows, cols), F32)
    half_norm = -0.5 * jnp.sum(jnp.transpose(norms[...]), axis=0, keepdims=True)
    half_norm = jnp.broadcast_to(half_norm, (8, cols))
    norm_row = jnp.zeros((8, cols), F32)
    product = lax.dot_general(moved[...], gathered[...], NT, preferred_element_type=F32)
    for q in range(pieces):
        scores += fold(q, product[q * cands:(q + 1) * cands])
        norm_row += fold(q, half_norm)
    column = lax.broadcasted_iota(jnp.int32, (rows, cols), 1)
    valid = (column & (TILE - 1)) < ref_rows
    blocks = []
    for t in range(SHIFTS):
        a, b = offsets(t)
        cost = (a * a + b * b).astype(F32) * PENALTY
        block = scores[t * rows:(t + 1) * rows] + norm_row[:1] - cost
        blocks.append(jnp.where(valid, block, -jnp.inf))
    top = functools.reduce(jnp.maximum, blocks)
    top = jnp.max(top, axis=1, keepdims=True)
    blocks = [jnp.exp(block - top) for block in blocks]
    total = jnp.sum(sum(blocks), axis=1, keepdims=True)
    inverse = 1.0 / total
    weights = jnp.concatenate([(block * inverse).astype(BF16) for block in blocks], axis=0)

    evidence = top + jnp.log(total)
    spot = lax.broadcasted_iota(jnp.int32, (rows, LANES), 0) + panel * rows
    log_row = jnp.sum(jnp.where(lane == spot, evidence, 0.0), axis=0, keepdims=True)
    logs[panel] = jnp.broadcast_to(log_row, (8, LANES))

    def log_copy(step):
        return pltpu.make_async_remote_copy(
            src_ref=logs.at[panel], dst_ref=logs.at[panel], send_sem=log_send.at[step - 1],
            recv_sem=log_recv.at[panel],
            device_id={"panel": lax.rem(panel + step, n_panel)}, device_id_type=MESH,
        )

    for step in range(1, n_panel):
        log_copy(step).start()

    mixed = lax.dot_general(onehot[...], weights, NT, preferred_element_type=F32).astype(BF16)

    chunk = 2 * LANES
    lines = seg_len // LANES
    for c in range(seg_len // chunk):
        total = jnp.zeros((block_total, chunk), F32)
        for s in range(segments):
            q, at = divmod(s * seg_len + c * chunk, width)
            total += jnp.dot(
                mixed[s * block_total:(s + 1) * block_total], moved[q * cands:(q + 1) * cands, at:at + chunk],
                preferred_element_type=F32,
            )
        for k in range(2):
            part32[pl.ds(2 * c + k, block_total, stride=lines), :] = total[:, k * LANES:(k + 1) * LANES]
    part16[...] = part32[...].astype(BF16)

    def tile_of(ref, d):
        return ref.at[pl.ds(pl.multiple_of(d * TILE, TILE), TILE), :]

    def part_copy(d):
        return pltpu.make_async_remote_copy(
            src_ref=tile_of(part16, d), dst_ref=tile_of(landed, me), send_sem=part_send,
            recv_sem=part_recv, device_id=place(d), device_id_type=MESH,
        )

    if n <= 16:
        for far_dom in range(n_dom - 1, -1, -1):
            for far_panel in range(n_panel):
                if far_dom or far_panel:
                    part_copy(
                        lax.rem(panel + far_panel, n_panel) * n_dom + lax.rem(dom + far_dom, n_dom)
                    ).start()
    else:
        @pl.loop(1, n)
        def _(o):
            part_copy(lax.rem(me + o, n)).start()

    own_at = pl.ds(pl.multiple_of(me * TILE, TILE), TILE)
    landed[own_at, :] = jnp.zeros((TILE, LANES), BF16)
    arrivals = pltpu.make_async_remote_copy(
        src_ref=part16.at[:(n - 1) * TILE, :], dst_ref=landed.at[:(n - 1) * TILE, :], send_sem=part_send,
        recv_sem=part_recv, device_id={"panel": sibling}, device_id_type=MESH,
    )
    arrivals.wait_recv()
    total = part32[own_at, :]
    for d in range(n):
        total += landed[d * TILE:(d + 1) * TILE, :].astype(F32)
    total = total * scale
    for k in range(TILE):
        vol_out[k // lines:k // lines + 1, (k % lines) * LANES:(k % lines + 1) * LANES] = total[k:k + 1]

    log_total = logs[panel]
    for step in range(1, n_panel):
        sender = lax.rem(panel + step, n_panel)
        pltpu.make_async_remote_copy(
            src_ref=logs.at[sender], dst_ref=logs.at[sender], send_sem=log_send.at[step - 1],
            recv_sem=log_recv.at[sender], device_id={"panel": sender}, device_id_type=MESH,
        ).wait_recv()
        log_total += logs[sender]
    log_out[...] = log_total[:1, :log_out.shape[1]]

    arrivals.wait_send()

    for step in range(1, n_panel):
        slot_copy(step).wait_send()
        log_copy(step).wait_send()
    for j in range(n_dom):
        @pl.when(j != dom)
        def _():
            line_copy(j).wait_send()

        for step in range(1, n_y):
            y_copy(step, j).wait_send()
        for step in range(n_y):
            sib_copy(y_peer(step) * n_dom + j).wait_send()


def shards(images, shift_index, references, slot_blocks):
    n_panel = lax.axis_size("panel")
    n_dom = lax.axis_size("dom")
    n = n_panel * n_dom
    part_dev, row_width = images.shape
    slot_rows, segments = slot_blocks.shape
    block_total = 2 * n
    volume_scale = (part_dev * n_dom * segments / block_total) ** (-0.5)
    rows = part_dev // n_panel
    width = row_width * references.shape[0] // TILE
    seg_len = row_width // segments
    lines = seg_len // LANES
    vmem = pl.BlockSpec(memory_space=pltpu.VMEM)
    dma = pltpu.SemaphoreType.DMA
    volume, log_evidence = pl.pallas_call(
        functools.partial(kernel, n_panel, n_dom, volume_scale),
        out_shape=(
            jax.ShapeDtypeStruct((2, seg_len), F32),
            jax.ShapeDtypeStruct((1, part_dev), F32),
        ),
        in_specs=[pl.BlockSpec(memory_space=pltpu.HBM)] * 4,
        out_specs=(vmem, vmem),
        scratch_shapes=[
            pltpu.VMEM((rows, row_width), BF16),
            pltpu.VMEM(references.shape, BF16),
            pltpu.VMEM((SHIFTS, part_dev), jnp.int32),
            pltpu.VMEM((TILE, LANES), F32),
            pltpu.VMEM((LANES, TILE), jnp.int32),
            pltpu.VMEM((TILE, width), F32),
            pltpu.VMEM((n * TILE, width), BF16),
            pltpu.VMEM((n * TILE, LANES), F32),
            pltpu.VMEM((SHIFTS * rows * (row_width // width), width), BF16),
            pltpu.VMEM((segments, slot_rows), jnp.int32),
            pltpu.VMEM((n_panel, segments, LANES), jnp.int32),
            pltpu.VMEM((segments * block_total, n * TILE), BF16),
            pltpu.VMEM((block_total * lines, LANES), F32),
            pltpu.VMEM((block_total * lines, LANES), BF16),
            pltpu.VMEM((n * TILE, LANES), BF16),
            pltpu.VMEM((n_panel, 8, LANES), F32),
            dma((4,)),
            dma((n,)),
            dma((n_dom,)),
            dma((max(n_panel // 2 - 1, 1), n_dom)),
            dma((n,)),
            dma((n_panel,)),
            dma((n_panel,)),
            dma(()),
            dma(()),
            dma((n_panel,)),
            dma((n_panel,)),
        ],
        compiler_params=pltpu.CompilerParams(
            collective_id=0, has_side_effects=True, vmem_limit_bytes=56 * 1024 * 1024
        ),
        name="expectation_backprojection",
    )(images, shift_index.T, references, slot_blocks.T)
    return volume, log_evidence.reshape(part_dev)


def solution(mesh):
    in_specs = (
        P(("half", "dom"), None),
        P(("half", "dom"), None),
        P(("half", "panel", "dom"), None),
        P(("half", "panel"), None),
    )
    out_specs = (P(("half", "panel", "dom"), None), P(("half", "dom")))
    return jax.shard_map(shards, mesh=mesh, in_specs=in_specs, out_specs=out_specs, check_vma=False)
```

```python
import functools
import math

import jax
import jax.numpy as jnp
from jax import lax
from jax.experimental import pallas as pl
from jax.experimental.pallas import tpu as pltpu
from jax.sharding import PartitionSpec as P

MESH = pl.DeviceIdType.MESH
PIX = 64
SHIFTS = 9
LANES = 128
TILE = 16
T_GROUP = 3
U_BLOCK = 8
HALVES = 2
PENALTY = 0.125
F32 = jnp.float32
BF16 = jnp.bfloat16
NT = (((1,), (1,)), ((), ()))


def row_offset(index):
    return (index * 37) >> 8


def kernel(
    n_panel, n_dom, scale, images, shift, refs, slots, vol_out, log_out,
    img, refs_in, shift_in, shift_pad, shift_col, refs32, gathered, norms, moved, slot_in, slot_all, onehot,
    part32, part16, landed, logs, in_sem, recv_sem, z_sem, y_sem, sib_sem, slot_send, slot_recv,
    part_send, part_recv, log_send, log_recv,
):
    n = n_panel * n_dom
    n_y = n_panel // 2
    panel, dom = lax.axis_index("panel"), lax.axis_index("dom")
    me = panel * n_dom + dom
    rows = img.shape[0]
    ref_rows = refs.shape[0]
    pieces = TILE // ref_rows
    width = gathered.shape[1]
    cols = gathered.shape[0]
    cands = SHIFTS * rows
    segments = slots.shape[0]
    seg_len = img.shape[1] // segments
    block_total = 2 * n
    core = lax.rem(panel, 2)
    sibling = panel + 1 - 2 * core

    def y_peer(step):
        return lax.rem(panel + 2 * step, n_panel)

    def place(d):
        return {"panel": lax.div(d, n_dom), "dom": lax.rem(d, n_dom)}

    barrier = pltpu.get_barrier_semaphore()

    @pl.loop(1, n_dom)
    def _(o):
        pl.semaphore_signal(
            barrier, inc=1, device_id={"dom": lax.rem(dom + o, n_dom)}, device_id_type=MESH
        )

    for step in range(1, n_panel):
        pl.semaphore_signal(
            barrier, inc=1, device_id={"panel": lax.rem(panel + step, n_panel)}, device_id_type=MESH
        )

    first = pl.multiple_of(panel * rows, rows)
    refs_copy = pltpu.make_async_copy(refs, refs_in, in_sem.at[0])
    img_copy = pltpu.make_async_copy(images.at[pl.ds(first, rows), :], img, in_sem.at[1])
    shift_copy = pltpu.make_async_copy(shift, shift_in, in_sem.at[2])
    slot_load = pltpu.make_async_copy(slots, slot_in, in_sem.at[3])
    refs_copy.start()
    shift_copy.start()
    slot_load.start()
    img_copy.start()

    half_width = width // HALVES

    def shard(d, h):
        return gathered.at[
            pl.ds(pl.multiple_of(d * TILE, TILE), TILE), h * half_width:(h + 1) * half_width
        ]

    def add_norm(d):
        at = pl.ds(pl.multiple_of(d * TILE, TILE), TILE)
        total = jnp.zeros((TILE, LANES), F32)
        for k in range(width // LANES):
            value = gathered[at, k * LANES:(k + 1) * LANES].astype(F32)
            total += value * value
        norms[at, :] = total

    refs_copy.wait()
    for q in range(pieces):
        refs32[q * ref_rows:(q + 1) * ref_rows, :] = refs_in[:, q * width:(q + 1) * width].astype(F32)
    gathered[pl.ds(pl.multiple_of(me * TILE, TILE), TILE), :] = refs32[...].astype(BF16)
    slot_load.wait()
    slot_all[panel] = jnp.zeros((segments, LANES), jnp.int32)
    slot_all[panel, :, :slots.shape[1]] = slot_in[...]

    pl.semaphore_wait(barrier, n_dom + n_panel - 2)

    def shard_copy(d, h, device, sem):
        return pltpu.make_async_remote_copy(
            src_ref=shard(d, h), dst_ref=shard(d, h), send_sem=sem, recv_sem=recv_sem.at[d, h],
            device_id=device, device_id_type=MESH,
        )

    def line_copy(target, h):
        return shard_copy(me, h, {"dom": target}, z_sem.at[target, h])

    def y_copy(step, j, h, cross=0):
        target = lax.rem(sibling + 2 * step, n_panel) if cross else y_peer(step)
        return shard_copy(panel * n_dom + j, h, {"panel": target}, y_sem.at[step - 1, j, 2 * h + cross])

    def sib_copy(d, h):
        return shard_copy(d, h, {"panel": sibling}, sib_sem.at[d, h])

    far = n_dom - 1 if n_dom > 1 else n_dom

    def at_distance(s, do):
        for h in range(HALVES):
            pl.when(dom - s >= 0)(functools.partial(do, dom - s, h))
            pl.when(dom + s < n_dom)(functools.partial(do, dom + s, h))

    def arrived(d, h):
        sib_copy(d, h).wait_recv()
        if h == HALVES - 1:
            add_norm(d)

    def from_line(s):
        def pass_on(j, h):
            sib_copy(panel * n_dom + j, h).wait_recv()
            for step in range(1, n_y):
                y_copy(step, j, h).start()
                if s == far:
                    y_copy(step, j, h, 1).start()
            sib_copy(panel * n_dom + j, h).start()
            if h == HALVES - 1:
                add_norm(panel * n_dom + j)

        at_distance(s, pass_on)

    def from_y(s):
        for step in range(1, n_y):
            base = y_peer(step) * n_dom

            def pass_on(j, h):
                sib_copy(base + j, h).wait_recv()
                if s != far:
                    sib_copy(base + j, h).start()
                if h == HALVES - 1:
                    add_norm(base + j)

            if s > 0:
                at_distance(s, pass_on)
            else:
                for h in range(HALVES):
                    pass_on(dom, h)

    def slot_copy(step):
        own = slot_all.at[panel]
        return pltpu.make_async_remote_copy(
            src_ref=own, dst_ref=own, send_sem=slot_send.at[step - 1], recv_sem=slot_recv.at[panel],
            device_id={"panel": lax.rem(panel + step, n_panel)}, device_id_type=MESH,
        )

    def send_line(s):
        at_distance(s, lambda target, h: line_copy(target, h).start())

    late = n_dom - 1 if n_dom > 3 else n_dom
    for s in range(1, late):
        send_line(s)
        if s == 1:
            for step in range(1, n_y):
                for h in range(HALVES):
                    y_copy(step, dom, h).start()
    for h in range(HALVES):
        sib_copy(me, h).start()
    for step in range(1, n_panel):
        slot_copy(step).start()

    lane = lax.broadcasted_iota(jnp.int32, (rows, LANES), 1)
    turn_sign = jnp.where(lane < PIX, -1.0, 1.0).astype(F32)
    freq_col = (lane & (PIX - 1)) - PIX // 2

    shift_copy.wait()
    shift_pad[...] = jnp.zeros(shift_pad.shape, F32)
    shift_pad[:SHIFTS, :shift.shape[1]] = shift_in[...].astype(F32)
    shift_col[...] = jnp.transpose(shift_pad[...]).astype(jnp.int32)

    multiple = lax.broadcasted_iota(jnp.int32, (8, LANES), 0)
    turns = (freq_col[:8] * multiple + PIX // 2) & (PIX - 1)
    angle = (turns - PIX // 2).astype(F32) * (-2.0 * math.pi / PIX)
    cos_rows, sin_rows = jnp.cos(angle), jnp.sin(angle)

    def offsets(t):
        index = shift_col[pl.ds(first, rows), t:t + 1]
        a = row_offset(index)
        return a - 3, index - 7 * a - 3

    def pick(k, options):
        out = options[0]
        for i in range(1, len(options)):
            out = jnp.where(k == i, options[i], out)
        return out

    blocks_per_piece = width // (U_BLOCK * LANES)

    def shift_group(t0):
        parts = []
        for t in range(t0, t0 + T_GROUP):
            a, b = offsets(t)
            a = jnp.broadcast_to(a, (rows, LANES))
            b = jnp.broadcast_to(b, (rows, LANES))
            flip = jnp.where((a & 1) == 1, -1.0, 1.0).astype(F32)
            far_a, far_b = jnp.abs(a), jnp.abs(b)
            cosine = flip * pick(far_b, [cos_rows[k:k + 1] for k in range(4)])
            sine = flip * pick(far_b, [sin_rows[k:k + 1] for k in range(4)]) * turn_sign
            sine = jnp.where(b < 0, -sine, sine)
            turn_cos = pick(far_a, [jnp.full((rows, LANES), math.cos(2 * math.pi * k / PIX), F32) for k in range(4)])
            turn_sin = pick(far_a, [jnp.full((rows, LANES), math.sin(2 * math.pi * k / PIX), F32) for k in range(4)])
            turn_sin = jnp.where(a < 0, turn_sin, -turn_sin) * turn_sign
            parts.append((cosine, sine, turn_cos, turn_sin))
        cosine, sine, turn_cos, turn_sin = (jnp.concatenate(x, axis=0) for x in zip(*parts))

        def body(block, carry):
            cosine, sine = carry
            q = lax.div(block, blocks_per_piece)
            lane0 = lax.rem(block, blocks_per_piece) * (U_BLOCK * LANES)
            at_rows = pl.ds(pl.multiple_of(q * cands + t0 * rows, rows), T_GROUP * rows)
            for k in range(U_BLOCK):
                at = pl.multiple_of((block * U_BLOCK + k) * LANES, LANES)
                to = pl.multiple_of(lane0 + k * LANES, LANES)
                x = img[:, pl.ds(at, LANES)].astype(F32)
                swapped = pltpu.roll(x, PIX, 1)
                x = jnp.concatenate([x] * T_GROUP, axis=0)
                swapped = jnp.concatenate([swapped] * T_GROUP, axis=0)
                moved[at_rows, pl.ds(to, LANES)] = (x * cosine + swapped * sine).astype(BF16)
                cosine, sine = cosine * turn_cos - sine * turn_sin, sine * turn_cos + cosine * turn_sin
            return cosine, sine

        lax.fori_loop(0, PIX // U_BLOCK, body, (cosine, sine))

    def build_onehot():
        for step in range(1, n_panel):
            sender = lax.rem(panel + step, n_panel)
            pltpu.make_async_remote_copy(
                src_ref=slot_all.at[sender], dst_ref=slot_all.at[sender], send_sem=slot_send.at[step - 1],
                recv_sem=slot_recv.at[sender], device_id={"panel": sender}, device_id_type=MESH,
            ).wait_recv()
        spread_col = lax.broadcasted_iota(jnp.int32, (LANES, cols), 1)
        spread_row = lax.broadcasted_iota(jnp.int32, (LANES, cols), 0)
        within = spread_col & (TILE - 1)
        spread_to = jnp.where(within < ref_rows, (spread_col >> 4) * ref_rows + within, -1)
        slot_of = jnp.zeros((segments, cols), F32)
        for k in range(n_panel):
            spread = jnp.where(spread_row + k * slots.shape[1] == spread_to, 1.0, 0.0)
            spread = jnp.where(spread_row < slots.shape[1], spread, 0.0).astype(BF16)
            slot_of += jnp.dot(slot_all[k].astype(F32).astype(BF16), spread, preferred_element_type=F32)
        block_id = lax.broadcasted_iota(jnp.int32, (block_total, cols), 0).astype(F32)
        for s in range(segments):
            onehot[s * block_total:(s + 1) * block_total, :] = jnp.where(
                block_id == slot_of[s:s + 1], 1.0, 0.0
            ).astype(BF16)

    img_copy.wait()
    for t0 in range(0, SHIFTS, T_GROUP):
        shift_group(t0)
    for s in range(late, n_dom):
        send_line(s)
    add_norm(me)
    for s in range(1, n_dom):
        from_line(s)
    build_onehot()
    for s in range(n_dom):
        from_y(s)
    for step in range(n_y):
        base = lax.rem(sibling + 2 * step, n_panel) * n_dom
        for j in range(n_dom):
            for h in range(HALVES):
                arrived(base + j, h)

    def fold(q, value):
        return value if q == 0 else pltpu.roll(value, cols - q * ref_rows, 1)

    scores = jnp.zeros((SHIFTS * rows, cols), F32)
    half_norm = -0.5 * jnp.sum(jnp.transpose(norms[...]), axis=0, keepdims=True)
    half_norm = jnp.broadcast_to(half_norm, (8, cols))
    norm_row = jnp.zeros((8, cols), F32)
    product = lax.dot_general(moved[...], gathered[...], NT, preferred_element_type=F32)
    for q in range(pieces):
        scores += fold(q, product[q * cands:(q + 1) * cands])
        norm_row += fold(q, half_norm)
    column = lax.broadcasted_iota(jnp.int32, (rows, cols), 1)
    valid = (column & (TILE - 1)) < ref_rows
    blocks = []
    for t in range(SHIFTS):
        a, b = offsets(t)
        cost = (a * a + b * b).astype(F32) * PENALTY
        block = scores[t * rows:(t + 1) * rows] + norm_row[:1] - cost
        blocks.append(jnp.where(valid, block, -jnp.inf))
    top = functools.reduce(jnp.maximum, blocks)
    top = jnp.max(top, axis=1, keepdims=True)
    blocks = [jnp.exp(block - top) for block in blocks]
    total = jnp.sum(sum(blocks), axis=1, keepdims=True)
    inverse = 1.0 / total
    weights = jnp.concatenate([(block * inverse).astype(BF16) for block in blocks], axis=0)

    evidence = top + jnp.log(total)
    spot = lax.broadcasted_iota(jnp.int32, (rows, LANES), 0) + panel * rows
    log_row = jnp.sum(jnp.where(lane == spot, evidence, 0.0), axis=0, keepdims=True)
    logs[panel] = jnp.broadcast_to(log_row, (8, LANES))

    def log_copy(step):
        return pltpu.make_async_remote_copy(
            src_ref=logs.at[panel], dst_ref=logs.at[panel], send_sem=log_send.at[step - 1],
            recv_sem=log_recv.at[panel],
            device_id={"panel": lax.rem(panel + step, n_panel)}, device_id_type=MESH,
        )

    for step in range(1, n_panel):
        log_copy(step).start()

    mixed = lax.dot_general(onehot[...], weights, NT, preferred_element_type=F32).astype(BF16)

    chunk = 2 * LANES
    lines = seg_len // LANES
    for c in range(seg_len // chunk):
        total = jnp.zeros((block_total, chunk), F32)
        for s in range(segments):
            q, at = divmod(s * seg_len + c * chunk, width)
            total += jnp.dot(
                mixed[s * block_total:(s + 1) * block_total], moved[q * cands:(q + 1) * cands, at:at + chunk],
                preferred_element_type=F32,
            )
        for k in range(2):
            part32[pl.ds(2 * c + k, block_total, stride=lines), :] = total[:, k * LANES:(k + 1) * LANES]
    part16[...] = part32[...].astype(BF16)

    def tile_of(ref, d):
        return ref.at[pl.ds(pl.multiple_of(d * TILE, TILE), TILE), :]

    def part_copy(d):
        return pltpu.make_async_remote_copy(
            src_ref=tile_of(part16, d), dst_ref=tile_of(landed, me), send_sem=part_send,
            recv_sem=part_recv, device_id=place(d), device_id_type=MESH,
        )

    if n <= 16:
        for far_dom in range(n_dom - 1, -1, -1):
            for far_panel in range(n_panel):
                if far_dom or far_panel:
                    part_copy(
                        lax.rem(panel + far_panel, n_panel) * n_dom + lax.rem(dom + far_dom, n_dom)
                    ).start()
    else:
        @pl.loop(1, n)
        def _(o):
            part_copy(lax.rem(me + o, n)).start()

    own_at = pl.ds(pl.multiple_of(me * TILE, TILE), TILE)
    landed[own_at, :] = jnp.zeros((TILE, LANES), BF16)
    arrivals = pltpu.make_async_remote_copy(
        src_ref=part16.at[:(n - 1) * TILE, :], dst_ref=landed.at[:(n - 1) * TILE, :], send_sem=part_send,
        recv_sem=part_recv, device_id={"panel": sibling}, device_id_type=MESH,
    )
    arrivals.wait_recv()
    total = part32[own_at, :]
    for d in range(n):
        total += landed[d * TILE:(d + 1) * TILE, :].astype(F32)
    total = total * scale
    for k in range(TILE):
        vol_out[k // lines:k // lines + 1, (k % lines) * LANES:(k % lines + 1) * LANES] = total[k:k + 1]

    log_total = logs[panel]
    for step in range(1, n_panel):
        sender = lax.rem(panel + step, n_panel)
        pltpu.make_async_remote_copy(
            src_ref=logs.at[sender], dst_ref=logs.at[sender], send_sem=log_send.at[step - 1],
            recv_sem=log_recv.at[sender], device_id={"panel": sender}, device_id_type=MESH,
        ).wait_recv()
        log_total += logs[sender]
    log_out[...] = log_total[:1, :log_out.shape[1]]

    arrivals.wait_send()

    for step in range(1, n_panel):
        slot_copy(step).wait_send()
        log_copy(step).wait_send()
    for j in range(n_dom):
        away = jnp.abs(dom - j)
        for h in range(HALVES):
            pl.when(away != 0)(lambda: line_copy(j, h).wait_send())
            sib_copy(panel * n_dom + j, h).wait_send()
            for step in range(1, n_y):
                y_copy(step, j, h).wait_send()
                pl.when(away == far)(lambda: y_copy(step, j, h, 1).wait_send())
                pl.when(away != far)(lambda: sib_copy(y_peer(step) * n_dom + j, h).wait_send())


def shards(images, shift_index, references, slot_blocks):
    n_panel = lax.axis_size("panel")
    n_dom = lax.axis_size("dom")
    n = n_panel * n_dom
    part_dev, row_width = images.shape
    slot_rows, segments = slot_blocks.shape
    block_total = 2 * n
    volume_scale = (part_dev * n_dom * segments / block_total) ** (-0.5)
    rows = part_dev // n_panel
    width = row_width * references.shape[0] // TILE
    seg_len = row_width // segments
    lines = seg_len // LANES
    vmem = pl.BlockSpec(memory_space=pltpu.VMEM)
    dma = pltpu.SemaphoreType.DMA
    volume, log_evidence = pl.pallas_call(
        functools.partial(kernel, n_panel, n_dom, volume_scale),
        out_shape=(
            jax.ShapeDtypeStruct((2, seg_len), F32),
            jax.ShapeDtypeStruct((1, part_dev), F32),
        ),
        in_specs=[pl.BlockSpec(memory_space=pltpu.HBM)] * 4,
        out_specs=(vmem, vmem),
        scratch_shapes=[
            pltpu.VMEM((rows, row_width), BF16),
            pltpu.VMEM(references.shape, BF16),
            pltpu.VMEM((SHIFTS, part_dev), jnp.int32),
            pltpu.VMEM((TILE, LANES), F32),
            pltpu.VMEM((LANES, TILE), jnp.int32),
            pltpu.VMEM((TILE, width), F32),
            pltpu.VMEM((n * TILE, width), BF16),
            pltpu.VMEM((n * TILE, LANES), F32),
            pltpu.VMEM((SHIFTS * rows * (row_width // width), width), BF16),
            pltpu.VMEM((segments, slot_rows), jnp.int32),
            pltpu.VMEM((n_panel, segments, LANES), jnp.int32),
            pltpu.VMEM((segments * block_total, n * TILE), BF16),
            pltpu.VMEM((block_total * lines, LANES), F32),
            pltpu.VMEM((block_total * lines, LANES), BF16),
            pltpu.VMEM((n * TILE, LANES), BF16),
            pltpu.VMEM((n_panel, 8, LANES), F32),
            dma((4,)),
            dma((n, HALVES)),
            dma((n_dom, HALVES)),
            dma((max(n_panel // 2 - 1, 1), n_dom, 2 * HALVES)),
            dma((n, HALVES)),
            dma((n_panel,)),
            dma((n_panel,)),
            dma(()),
            dma(()),
            dma((n_panel,)),
            dma((n_panel,)),
        ],
        compiler_params=pltpu.CompilerParams(
            collective_id=0, has_side_effects=True, vmem_limit_bytes=56 * 1024 * 1024
        ),
        name="expectation_backprojection",
    )(images, shift_index.T, references, slot_blocks.T)
    return volume, log_evidence.reshape(part_dev)


def solution(mesh):
    in_specs = (
        P(("half", "dom"), None),
        P(("half", "dom"), None),
        P(("half", "panel", "dom"), None),
        P(("half", "panel"), None),
    )
    out_specs = (P(("half", "panel", "dom"), None), P(("half", "dom")))
    return jax.shard_map(shards, mesh=mesh, in_specs=in_specs, out_specs=out_specs, check_vma=False)
```

```python
import functools
import math

import jax
import jax.numpy as jnp
from jax import lax
from jax.experimental import pallas as pl
from jax.experimental.pallas import tpu as pltpu
from jax.sharding import PartitionSpec as P

MESH = pl.DeviceIdType.MESH
PIX = 64
SHIFTS = 9
LANES = 128
TILE = 16
T_GROUP = 3
U_BLOCK = 8
PENALTY = 0.125
F32 = jnp.float32
BF16 = jnp.bfloat16
NT = (((1,), (1,)), ((), ()))


def row_offset(index):
    return (index * 37) >> 8


def kernel(
    n_panel, n_dom, scale, images, shift, refs, slots, vol_out, log_out,
    img, refs_in, shift_in, shift_pad, shift_col, refs32, gathered, norms, moved, slot_in, slot_all, onehot,
    part32, part16, landed, logs, in_sem, recv_sem, z_sem, y_sem, sib_sem, slot_send, slot_recv,
    part_send, part_recv, log_send, log_recv,
):
    n = n_panel * n_dom
    n_y = n_panel // 2
    panel, dom = lax.axis_index("panel"), lax.axis_index("dom")
    me = panel * n_dom + dom
    rows = img.shape[0]
    ref_rows = refs.shape[0]
    pieces = TILE // ref_rows
    width = gathered.shape[1]
    cols = gathered.shape[0]
    cands = SHIFTS * rows
    segments = slots.shape[0]
    seg_len = img.shape[1] // segments
    block_total = 2 * n
    core = lax.rem(panel, 2)
    sibling = panel + 1 - 2 * core

    def y_peer(step):
        return lax.rem(panel + 2 * step, n_panel)

    def place(d):
        return {"panel": lax.div(d, n_dom), "dom": lax.rem(d, n_dom)}

    barrier = pltpu.get_barrier_semaphore()

    @pl.loop(1, n_dom)
    def _(o):
        pl.semaphore_signal(
            barrier, inc=1, device_id={"dom": lax.rem(dom + o, n_dom)}, device_id_type=MESH
        )

    for step in range(1, n_panel):
        pl.semaphore_signal(
            barrier, inc=1, device_id={"panel": lax.rem(panel + step, n_panel)}, device_id_type=MESH
        )

    first = pl.multiple_of(panel * rows, rows)
    refs_copy = pltpu.make_async_copy(refs, refs_in, in_sem.at[0])
    img_copy = pltpu.make_async_copy(images.at[pl.ds(first, rows), :], img, in_sem.at[1])
    shift_copy = pltpu.make_async_copy(shift, shift_in, in_sem.at[2])
    slot_load = pltpu.make_async_copy(slots, slot_in, in_sem.at[3])
    refs_copy.start()
    shift_copy.start()
    slot_load.start()
    img_copy.start()

    def shard(d):
        return gathered.at[pl.ds(pl.multiple_of(d * TILE, TILE), TILE), :]

    def add_norm(d):
        at = pl.ds(pl.multiple_of(d * TILE, TILE), TILE)
        total = jnp.zeros((TILE, LANES), F32)
        for k in range(width // LANES):
            value = gathered[at, k * LANES:(k + 1) * LANES].astype(F32)
            total += value * value
        norms[at, :] = total

    lane = lax.broadcasted_iota(jnp.int32, (rows, LANES), 1)
    turn_sign = jnp.where(lane < PIX, -1.0, 1.0).astype(F32)
    freq_col = (lane & (PIX - 1)) - PIX // 2

    shift_copy.wait()
    shift_pad[...] = jnp.zeros(shift_pad.shape, F32)
    shift_pad[:SHIFTS, :shift.shape[1]] = shift_in[...].astype(F32)
    shift_col[...] = jnp.transpose(shift_pad[...]).astype(jnp.int32)

    multiple = lax.broadcasted_iota(jnp.int32, (8, LANES), 0)
    turns = (freq_col[:8] * multiple + PIX // 2) & (PIX - 1)
    angle = (turns - PIX // 2).astype(F32) * (-2.0 * math.pi / PIX)
    cos_rows, sin_rows = jnp.cos(angle), jnp.sin(angle)

    refs_copy.wait()
    for q in range(pieces):
        refs32[q * ref_rows:(q + 1) * ref_rows, :] = refs_in[:, q * width:(q + 1) * width].astype(F32)
    gathered[pl.ds(pl.multiple_of(me * TILE, TILE), TILE), :] = refs32[...].astype(BF16)
    slot_load.wait()
    slot_all[panel] = jnp.zeros((segments, LANES), jnp.int32)
    slot_all[panel, :, :slots.shape[1]] = slot_in[...]

    pl.semaphore_wait(barrier, n_dom + n_panel - 2)

    def shard_copy(d, device, sem):
        return pltpu.make_async_remote_copy(
            src_ref=shard(d), dst_ref=shard(d), send_sem=sem, recv_sem=recv_sem.at[d],
            device_id=device, device_id_type=MESH,
        )

    def line_copy(target):
        return shard_copy(me, {"dom": target}, z_sem.at[target])

    def y_copy(step, j):
        return shard_copy(panel * n_dom + j, {"panel": y_peer(step)}, y_sem.at[step - 1, j])

    def sib_copy(d):
        return shard_copy(d, {"panel": sibling}, sib_sem.at[d])

    def relay(j):
        for step in range(1, n_y):
            y_copy(step, j).start()
        sib_copy(panel * n_dom + j).start()

    def from_line(j):
        sib_copy(panel * n_dom + j).wait_recv()
        relay(j)
        add_norm(panel * n_dom + j)

    def at_distance(s, do):
        pl.when(dom - s >= 0)(lambda: do(dom - s))
        pl.when(dom + s < n_dom)(lambda: do(dom + s))

    def from_y(s):
        for step in range(1, n_y):
            base = y_peer(step) * n_dom

            def pass_on(j):
                sib_copy(base + j).wait_recv()
                sib_copy(base + j).start()
                add_norm(base + j)

            if s > 0:
                at_distance(s, pass_on)
            else:
                pass_on(dom)

    def slot_copy(step):
        own = slot_all.at[panel]
        return pltpu.make_async_remote_copy(
            src_ref=own, dst_ref=own, send_sem=slot_send.at[step - 1], recv_sem=slot_recv.at[panel],
            device_id={"panel": lax.rem(panel + step, n_panel)}, device_id_type=MESH,
        )

    def send_line(s):
        at_distance(s, lambda target: line_copy(target).start())

    late = n_dom - 1 if n_dom > 3 else n_dom
    for s in range(1, late):
        send_line(s)
        if s == 1:
            for step in range(1, n_y):
                y_copy(step, dom).start()
    sib_copy(me).start()
    for step in range(1, n_panel):
        slot_copy(step).start()

    def offsets(t):
        index = shift_col[pl.ds(first, rows), t:t + 1]
        a = row_offset(index)
        return a - 3, index - 7 * a - 3

    def pick(k, options):
        out = options[0]
        for i in range(1, len(options)):
            out = jnp.where(k == i, options[i], out)
        return out

    blocks_per_piece = width // (U_BLOCK * LANES)

    def shift_group(t0):
        parts = []
        for t in range(t0, t0 + T_GROUP):
            a, b = offsets(t)
            a = jnp.broadcast_to(a, (rows, LANES))
            b = jnp.broadcast_to(b, (rows, LANES))
            flip = jnp.where((a & 1) == 1, -1.0, 1.0).astype(F32)
            far_a, far_b = jnp.abs(a), jnp.abs(b)
            cosine = flip * pick(far_b, [cos_rows[k:k + 1] for k in range(4)])
            sine = flip * pick(far_b, [sin_rows[k:k + 1] for k in range(4)]) * turn_sign
            sine = jnp.where(b < 0, -sine, sine)
            turn_cos = pick(far_a, [jnp.full((rows, LANES), math.cos(2 * math.pi * k / PIX), F32) for k in range(4)])
            turn_sin = pick(far_a, [jnp.full((rows, LANES), math.sin(2 * math.pi * k / PIX), F32) for k in range(4)])
            turn_sin = jnp.where(a < 0, turn_sin, -turn_sin) * turn_sign
            parts.append((cosine, sine, turn_cos, turn_sin))
        cosine, sine, turn_cos, turn_sin = (jnp.concatenate(x, axis=0) for x in zip(*parts))

        def body(block, carry):
            cosine, sine = carry
            q = lax.div(block, blocks_per_piece)
            lane0 = lax.rem(block, blocks_per_piece) * (U_BLOCK * LANES)
            at_rows = pl.ds(pl.multiple_of(q * cands + t0 * rows, rows), T_GROUP * rows)
            for k in range(U_BLOCK):
                at = pl.multiple_of((block * U_BLOCK + k) * LANES, LANES)
                to = pl.multiple_of(lane0 + k * LANES, LANES)
                x = img[:, pl.ds(at, LANES)].astype(F32)
                swapped = pltpu.roll(x, PIX, 1)
                x = jnp.concatenate([x] * T_GROUP, axis=0)
                swapped = jnp.concatenate([swapped] * T_GROUP, axis=0)
                moved[at_rows, pl.ds(to, LANES)] = (x * cosine + swapped * sine).astype(BF16)
                cosine, sine = cosine * turn_cos - sine * turn_sin, sine * turn_cos + cosine * turn_sin
            return cosine, sine

        lax.fori_loop(0, PIX // U_BLOCK, body, (cosine, sine))

    def build_onehot():
        for step in range(1, n_panel):
            sender = lax.rem(panel + step, n_panel)
            pltpu.make_async_remote_copy(
                src_ref=slot_all.at[sender], dst_ref=slot_all.at[sender], send_sem=slot_send.at[step - 1],
                recv_sem=slot_recv.at[sender], device_id={"panel": sender}, device_id_type=MESH,
            ).wait_recv()
        spread_col = lax.broadcasted_iota(jnp.int32, (LANES, cols), 1)
        spread_row = lax.broadcasted_iota(jnp.int32, (LANES, cols), 0)
        within = spread_col & (TILE - 1)
        spread_to = jnp.where(within < ref_rows, (spread_col >> 4) * ref_rows + within, -1)
        slot_of = jnp.zeros((segments, cols), F32)
        for k in range(n_panel):
            spread = jnp.where(spread_row + k * slots.shape[1] == spread_to, 1.0, 0.0)
            spread = jnp.where(spread_row < slots.shape[1], spread, 0.0).astype(BF16)
            slot_of += jnp.dot(slot_all[k].astype(F32).astype(BF16), spread, preferred_element_type=F32)
        block_id = lax.broadcasted_iota(jnp.int32, (block_total, cols), 0).astype(F32)
        for s in range(segments):
            onehot[s * block_total:(s + 1) * block_total, :] = jnp.where(
                block_id == slot_of[s:s + 1], 1.0, 0.0
            ).astype(BF16)

    img_copy.wait()
    shift_group(0)
    for s in range(late, n_dom):
        send_line(s)
    for t0 in range(T_GROUP, SHIFTS, T_GROUP):
        shift_group(t0)
    add_norm(me)
    for s in range(1, n_dom):
        at_distance(s, from_line)
    build_onehot()
    for s in range(n_dom):
        from_y(s)
    for step in range(n_y):
        base = lax.rem(sibling + 2 * step, n_panel) * n_dom
        for j in range(n_dom):
            sib_copy(base + j).wait_recv()
            add_norm(base + j)

    def fold(q, value):
        return value if q == 0 else pltpu.roll(value, cols - q * ref_rows, 1)

    scores = jnp.zeros((SHIFTS * rows, cols), F32)
    half_norm = -0.5 * jnp.sum(jnp.transpose(norms[...]), axis=0, keepdims=True)
    half_norm = jnp.broadcast_to(half_norm, (8, cols))
    norm_row = jnp.zeros((8, cols), F32)
    product = lax.dot_general(moved[...], gathered[...], NT, preferred_element_type=F32)
    for q in range(pieces):
        scores += fold(q, product[q * cands:(q + 1) * cands])
        norm_row += fold(q, half_norm)
    column = lax.broadcasted_iota(jnp.int32, (rows, cols), 1)
    valid = (column & (TILE - 1)) < ref_rows
    blocks = []
    for t in range(SHIFTS):
        a, b = offsets(t)
        cost = (a * a + b * b).astype(F32) * PENALTY
        block = scores[t * rows:(t + 1) * rows] + norm_row[:1] - cost
        blocks.append(jnp.where(valid, block, -jnp.inf))
    top = functools.reduce(jnp.maximum, blocks)
    top = jnp.max(top, axis=1, keepdims=True)
    blocks = [jnp.exp(block - top) for block in blocks]
    total = jnp.sum(sum(blocks), axis=1, keepdims=True)
    inverse = 1.0 / total
    weights = jnp.concatenate([(block * inverse).astype(BF16) for block in blocks], axis=0)

    evidence = top + jnp.log(total)
    spot = lax.broadcasted_iota(jnp.int32, (rows, LANES), 0) + panel * rows
    log_row = jnp.sum(jnp.where(lane == spot, evidence, 0.0), axis=0, keepdims=True)
    logs[panel] = jnp.broadcast_to(log_row, (8, LANES))

    def log_copy(step):
        return pltpu.make_async_remote_copy(
            src_ref=logs.at[panel], dst_ref=logs.at[panel], send_sem=log_send.at[step - 1],
            recv_sem=log_recv.at[panel],
            device_id={"panel": lax.rem(panel + step, n_panel)}, device_id_type=MESH,
        )

    for step in range(1, n_panel):
        log_copy(step).start()

    mixed = lax.dot_general(onehot[...], weights, NT, preferred_element_type=F32).astype(BF16)

    chunk = 2 * LANES
    lines = seg_len // LANES
    for c in range(seg_len // chunk):
        total = jnp.zeros((block_total, chunk), F32)
        for s in range(segments):
            q, at = divmod(s * seg_len + c * chunk, width)
            total += jnp.dot(
                mixed[s * block_total:(s + 1) * block_total], moved[q * cands:(q + 1) * cands, at:at + chunk],
                preferred_element_type=F32,
            )
        for k in range(2):
            part32[pl.ds(2 * c + k, block_total, stride=lines), :] = total[:, k * LANES:(k + 1) * LANES]
    part16[...] = part32[...].astype(BF16)

    def tile_of(ref, d):
        return ref.at[pl.ds(pl.multiple_of(d * TILE, TILE), TILE), :]

    def part_copy(d):
        return pltpu.make_async_remote_copy(
            src_ref=tile_of(part16, d), dst_ref=tile_of(landed, me), send_sem=part_send,
            recv_sem=part_recv, device_id=place(d), device_id_type=MESH,
        )

    if n <= 16:
        for far_dom in range(n_dom - 1, -1, -1):
            for far_panel in range(n_panel):
                if far_dom or far_panel:
                    part_copy(
                        lax.rem(panel + far_panel, n_panel) * n_dom + lax.rem(dom + far_dom, n_dom)
                    ).start()
    else:
        @pl.loop(1, n)
        def _(o):
            part_copy(lax.rem(me + o, n)).start()

    own_at = pl.ds(pl.multiple_of(me * TILE, TILE), TILE)
    landed[own_at, :] = jnp.zeros((TILE, LANES), BF16)
    arrivals = pltpu.make_async_remote_copy(
        src_ref=part16.at[:(n - 1) * TILE, :], dst_ref=landed.at[:(n - 1) * TILE, :], send_sem=part_send,
        recv_sem=part_recv, device_id={"panel": sibling}, device_id_type=MESH,
    )
    arrivals.wait_recv()
    total = part32[own_at, :]
    for d in range(n):
        total += landed[d * TILE:(d + 1) * TILE, :].astype(F32)
    total = total * scale
    for k in range(TILE):
        vol_out[k // lines:k // lines + 1, (k % lines) * LANES:(k % lines + 1) * LANES] = total[k:k + 1]

    log_total = logs[panel]
    for step in range(1, n_panel):
        sender = lax.rem(panel + step, n_panel)
        pltpu.make_async_remote_copy(
            src_ref=logs.at[sender], dst_ref=logs.at[sender], send_sem=log_send.at[step - 1],
            recv_sem=log_recv.at[sender], device_id={"panel": sender}, device_id_type=MESH,
        ).wait_recv()
        log_total += logs[sender]
    log_out[...] = log_total[:1, :log_out.shape[1]]

    arrivals.wait_send()

    for step in range(1, n_panel):
        slot_copy(step).wait_send()
        log_copy(step).wait_send()
    for j in range(n_dom):
        @pl.when(j != dom)
        def _():
            line_copy(j).wait_send()

        for step in range(1, n_y):
            y_copy(step, j).wait_send()
        for step in range(n_y):
            sib_copy(y_peer(step) * n_dom + j).wait_send()


def shards(images, shift_index, references, slot_blocks):
    n_panel = lax.axis_size("panel")
    n_dom = lax.axis_size("dom")
    n = n_panel * n_dom
    part_dev, row_width = images.shape
    slot_rows, segments = slot_blocks.shape
    block_total = 2 * n
    volume_scale = (part_dev * n_dom * segments / block_total) ** (-0.5)
    rows = part_dev // n_panel
    width = row_width * references.shape[0] // TILE
    seg_len = row_width // segments
    lines = seg_len // LANES
    vmem = pl.BlockSpec(memory_space=pltpu.VMEM)
    dma = pltpu.SemaphoreType.DMA
    volume, log_evidence = pl.pallas_call(
        functools.partial(kernel, n_panel, n_dom, volume_scale),
        out_shape=(
            jax.ShapeDtypeStruct((2, seg_len), F32),
            jax.ShapeDtypeStruct((1, part_dev), F32),
        ),
        in_specs=[pl.BlockSpec(memory_space=pltpu.HBM)] * 4,
        out_specs=(vmem, vmem),
        scratch_shapes=[
            pltpu.VMEM((rows, row_width), BF16),
            pltpu.VMEM(references.shape, BF16),
            pltpu.VMEM((SHIFTS, part_dev), jnp.int32),
            pltpu.VMEM((TILE, LANES), F32),
            pltpu.VMEM((LANES, TILE), jnp.int32),
            pltpu.VMEM((TILE, width), F32),
            pltpu.VMEM((n * TILE, width), BF16),
            pltpu.VMEM((n * TILE, LANES), F32),
            pltpu.VMEM((SHIFTS * rows * (row_width // width), width), BF16),
            pltpu.VMEM((segments, slot_rows), jnp.int32),
            pltpu.VMEM((n_panel, segments, LANES), jnp.int32),
            pltpu.VMEM((segments * block_total, n * TILE), BF16),
            pltpu.VMEM((block_total * lines, LANES), F32),
            pltpu.VMEM((block_total * lines, LANES), BF16),
            pltpu.VMEM((n * TILE, LANES), BF16),
            pltpu.VMEM((n_panel, 8, LANES), F32),
            dma((4,)),
            dma((n,)),
            dma((n_dom,)),
            dma((max(n_panel // 2 - 1, 1), n_dom)),
            dma((n,)),
            dma((n_panel,)),
            dma((n_panel,)),
            dma(()),
            dma(()),
            dma((n_panel,)),
            dma((n_panel,)),
        ],
        compiler_params=pltpu.CompilerParams(
            collective_id=0, has_side_effects=True, vmem_limit_bytes=56 * 1024 * 1024
        ),
        name="expectation_backprojection",
    )(images, shift_index.T, references, slot_blocks.T)
    return volume, log_evidence.reshape(part_dev)


def solution(mesh):
    in_specs = (
        P(("half", "dom"), None),
        P(("half", "dom"), None),
        P(("half", "panel", "dom"), None),
        P(("half", "panel"), None),
    )
    out_specs = (P(("half", "panel", "dom"), None), P(("half", "dom")))
    return jax.shard_map(shards, mesh=mesh, in_specs=in_specs, out_specs=out_specs, check_vma=False)
```
